256 devices in a mesh: pipe: 8 (over x, core), expert: 32 (over y, z).
Axes of the slice: x: 4, y: 4, z: 8, core: 2. Of those that a mesh axis runs over, the one named last changes fastest.
Arguments:
- tokens: bfloat16 [8, 4096, 3584], P('pipe', 'expert'), may hold values from -6 to 6
- expert_ids: int32 [8, 4096, 1], P('pipe', 'expert'), may hold values from 0 to 3; in each aligned block of 128 rows (0 to 127, 128 to 255, ..., all dimensions but the last counted through in order) at most 33 rows name the same one
- route_weight: bfloat16 [8, 4096, 1], P('pipe', 'expert'), may hold values from 0.049804688 to 0.5
- cotangent: bfloat16 [8, 4096, 3584], P('pipe', 'expert'), may hold values from -1.5 to 1.5
- w_gate: bfloat16 [8, 3584, 4096], P('pipe', None, 'expert'), as said below
- w_up: bfloat16 [8, 3584, 4096], P('pipe', None, 'expert'), as said below
- w_down: bfloat16 [8, 4096, 3584], P('pipe', 'expert'), as said below
Outputs:
- token_grad: bfloat16 [8, 4096, 3584], P('pipe', 'expert')
- route_grad: bfloat16 [8, 4096, 1], P('pipe', 'expert')
- grad_gate: bfloat16 [8, 3584, 4096], P('pipe', None, 'expert')
- grad_up: bfloat16 [8, 3584, 4096], P('pipe', None, 'expert')
- grad_down: bfloat16 [8, 4096, 3584], P('pipe', 'expert')
The draws below stay inside these ranges and needn't reach their ends.
Inputs may be any that keep to these rules, and one draw needn't show every extreme that they name: `expert_ids`: each token names one expert; among one device's 128 tokens no expert is named more than 33 times, a bound that some block reaches. `w_gate`: the copies of ranks 2j and 2j + 1 are equal. `w_up`: the copies of ranks 2j and 2j + 1 are equal. `w_down`: the copies of ranks 2j and 2j + 1 are equal.
All inputs are finite; a program needn't handle non-finite values.
Results may differ from the reference program's by a relative error of at most 0.0065.
Values may be sent and summed in bfloat16 or wider, within the bound.
A program may use at most 128 MiB of HBM per device.

```python
import math
from functools import partial
import jax
import jax.numpy as jnp
import numpy as np
from jax import lax

D = 3584
HID = 1024
EXPERTS = 4
TOP = 1
TOK_DEV = 128
GROUP = 8
HID_DEV = 128
TOKENS = 4096
CAP = 33
N_PIPE = 8
N_EXPERT = 32


def paired_copies(half):
    return jnp.repeat(half, 2, axis=0).astype(jnp.bfloat16)


def draw_w_gate(key, part):
    key = jax.random.fold_in(key, 11)
    half = jax.random.normal(key, (N_PIPE // 2, D, EXPERTS * HID), jnp.float32)
    return paired_copies(half * D ** (-0.5))


def draw_w_up(key, part):
    key = jax.random.fold_in(key, 23)
    half = jax.random.normal(key, (N_PIPE // 2, D, EXPERTS * HID), jnp.float32)
    return paired_copies(half * D ** (-0.5))


def draw_w_down(key, part):
    key = jax.random.fold_in(key, 37)
    half = jax.random.normal(key, (N_PIPE // 2, EXPERTS * HID, D), jnp.float32)
    return paired_copies(half * HID ** (-0.5))


def block_scale(own_key, extent, split, smallest, high):
    gain = 1.0
    for dim, shards_of in split:
        draws = jax.random.uniform(jax.random.fold_in(jax.random.fold_in(own_key, 6), dim), (shards_of,), jnp.float32, smallest / len(split), high / len(split))
        gain = gain * jnp.repeat(jnp.exp(draws), extent[dim] // shards_of).reshape((-1,) + (1,) * (len(extent) - 1 - dim))
    return gain


def shared_out(key, own, number, rows, number_of, top, most, lean):
    ranking = jax.random.permutation(key, number_of)
    packed, common = portions_of(number_of, rows * top, most, lean, True), portions_of(number_of, rows * top, most, lean, False)
    places = jnp.arange(number_of)

    def named(tallies, offset_by):
        used = int((tallies > 0).sum())
        fixed = max(1, used // 4)
        moved = fixed + (places - fixed + offset_by * (used - fixed)) % max(1, number_of - fixed)
        return jnp.zeros((number_of,), jnp.int32).at[ranking[jnp.where(places < fixed, places, moved)]].set(jnp.asarray(tallies, jnp.int32))

    tallies = jnp.where(number % 4 == 0, named(packed, number // 4), named(common, number - number // 4 - 1))
    mixed = jax.random.permutation(jax.random.fold_in(own, 3), number_of)
    source_of, receiver = mixed[0:number_of // 2 * 2:2], mixed[1:number_of // 2 * 2:2]
    room = jnp.minimum(tallies[source_of] - 1, most - tallies[receiver]) // 2
    room = jnp.where((source_of == ranking[0]) | (receiver == ranking[0]) | (tallies[receiver] == 0), 0, jnp.maximum(room, 0))
    moved = jax.random.randint(jax.random.fold_in(own, 4), (number_of // 2,), 0, 1 << 20) % (room + 1)
    tallies = tallies.at[source_of].add(-moved).at[receiver].add(moved)
    items = jnp.searchsorted(jnp.cumsum(tallies), jnp.arange(rows * top), side="right").astype(jnp.int32)
    table = items.reshape(top, rows).T
    table = table[jax.random.permutation(jax.random.fold_in(own, 1), rows)]
    offset_by = jax.random.randint(jax.random.fold_in(own, 2), (rows, 1), 0, top)
    return jnp.take_along_axis(table, (jnp.arange(top)[None, :] + offset_by) % top, axis=1)


def portions_of(number_of, total, bound, slope, full):
    weights = [(1 << 20) // math.isqrt(grade ** slope) + 1 for grade in range(1, number_of + 1)]
    largest = bound if full else min(bound, max(-(-total // number_of), total * weights[0] // sum(weights)))
    least = 1 if total - largest >= number_of - 1 else 0
    holding, rest = [largest] + [least] * (number_of - 1), total - largest - least * (number_of - 1)
    while rest > 0:
        free = [i for i in range(1, number_of) if holding[i] < largest] or [i for i in range(1, number_of) if holding[i] < bound]
        whole, budget = sum([weights[i] for i in free]), rest
        for i in free:
            extra = min(bound - holding[i], max(1, budget * weights[i] // whole), rest)
            holding[i] = holding[i] + extra
            rest = rest - extra
    return np.array(holding)


def noise(own_key, dims, deviation, reach, shards=(), kind=jnp.bfloat16):
    values = deviation * jax.random.normal(own_key, dims, jnp.float32)
    if shards:
        values = values * block_scale(own_key, dims, shards, -0.22, 0.18)
    return jnp.clip(values, -reach, reach).astype(kind)


def setup_inputs(seed: int = 0) -> dict:
    seeds = jax.random.split(jax.random.key(seed), 8)
    tokens = noise(seeds[0], (N_PIPE, TOKENS, D), 1.0, 6.0, ((0, 8), (1, 32)))
    expert_ids_keys = jax.random.split(jax.random.fold_in(seeds[1], 1), N_PIPE * TOKENS // TOK_DEV)
    expert_ids_turns = jax.random.permutation(jax.random.fold_in(seeds[1], 3), N_PIPE * TOKENS // TOK_DEV)
    expert_ids = jax.vmap(lambda own, number: shared_out(jax.random.fold_in(seeds[1], 2), own, number, TOK_DEV, EXPERTS, TOP, CAP, 1))(expert_ids_keys, expert_ids_turns).reshape((N_PIPE, TOKENS, TOP))
    route_weight = jnp.clip(jnp.exp(math.log(0.5) - 2.306499 * jax.random.uniform(seeds[2], (N_PIPE, TOKENS, TOP), jnp.float32) ** block_scale(seeds[2], (N_PIPE, TOKENS, TOP), ((0, 8), (1, 32)), -0.2, 0.2)), 0.049804688, 0.5).astype(jnp.bfloat16)
    cotangent = noise(seeds[3], (N_PIPE, TOKENS, D), 0.25, 1.5, ((0, 8), (1, 32)))
    w_gate = draw_w_gate(jax.random.fold_in(seeds[7], 71), 0)
    w_up = draw_w_up(jax.random.fold_in(seeds[7], 71), 0)
    w_down = draw_w_down(jax.random.fold_in(seeds[7], 71), 0)
    return {"tokens": tokens, "expert_ids": expert_ids, "route_weight": route_weight, "cotangent": cotangent, "w_gate": w_gate, "w_up": w_up, "w_down": w_down}


def make_slots(block_ids, experts, capacity):
    flat_ids = block_ids.reshape(-1).astype(jnp.int32)
    onehot = (flat_ids[:, None] == jnp.arange(experts, dtype=jnp.int32)[None, :]).astype(jnp.int32)
    running = jnp.cumsum(onehot, axis=0) * onehot
    target_slot = (flat_ids * capacity + jnp.sum(running, axis=1) - 1).astype(jnp.int32)
    positions = jnp.arange(flat_ids.shape[0], dtype=jnp.int32)
    source_row = jnp.full((experts * capacity,), -1, jnp.int32).at[target_slot].set(positions)
    return source_row, target_slot


def pack_rows(source_row, values, top_count):
    filled = source_row >= 0
    picked = values[(jnp.maximum(source_row, 0) // top_count).astype(jnp.int32)]
    return jnp.where(filled[:, None], picked, jnp.zeros_like(picked))


def pack_weights(source_row, route_block):
    filled = source_row >= 0
    picked = route_block.reshape(-1)[jnp.maximum(source_row, 0).astype(jnp.int32)]
    return jnp.where(filled, picked, jnp.zeros_like(picked))


def contract_rows(left, right):
    return lax.dot_general(left, right, (((0,), (0,)), ((), ())), preferred_element_type=jnp.float32)


def contract_cols(left, right):
    return lax.dot_general(left, right, (((1,), (1,)), ((), ())), preferred_element_type=jnp.float32)


def expert_forward(recv_rows, gate_weight, up_weight, down_weight):
    gate_pre = jnp.dot(recv_rows, gate_weight, preferred_element_type=jnp.float32)
    up_pre = jnp.dot(recv_rows, up_weight, preferred_element_type=jnp.float32)
    gate_sig = jax.nn.sigmoid(gate_pre)
    hidden = (gate_pre * gate_sig * up_pre).astype(jnp.bfloat16)
    expert_out = jnp.dot(hidden, down_weight, preferred_element_type=jnp.float32)
    return gate_pre, up_pre, hidden, expert_out


def expert_backward(recv_rows, slot_weight, cot_rows, saved_state, gate_weight, up_weight, down_weight):
    gate_pre, up_pre, hidden, expert_out = saved_state
    cot_wide = cot_rows.astype(jnp.float32)
    scaled = (slot_weight.astype(jnp.float32)[:, None] * cot_wide).astype(jnp.bfloat16)
    slot_grad = jnp.sum(expert_out * cot_wide, axis=1).astype(jnp.bfloat16)
    hidden_grad = contract_cols(scaled, down_weight)
    gate_sig = jax.nn.sigmoid(gate_pre)
    grad_gate_pre = (hidden_grad * up_pre * gate_sig * (1.0 + gate_pre * (1.0 - gate_sig))).astype(jnp.bfloat16)
    grad_up_pre = (hidden_grad * gate_pre * gate_sig).astype(jnp.bfloat16)
    row_grad = (contract_cols(grad_gate_pre, gate_weight) + contract_cols(grad_up_pre, up_weight)).astype(jnp.bfloat16)
    gate_term = contract_rows(recv_rows, grad_gate_pre).astype(jnp.bfloat16)
    up_term = contract_rows(recv_rows, grad_up_pre).astype(jnp.bfloat16)
    down_term = contract_rows(hidden, scaled).astype(jnp.bfloat16)
    return row_grad, slot_grad, gate_term, up_term, down_term


def per_piece(operands, rows_experts, weights_experts, cots_experts):
    expert_index, gate_weight, up_weight, down_weight = operands
    recv_rows = lax.dynamic_index_in_dim(rows_experts, expert_index, 0, keepdims=False)
    slot_weight = lax.dynamic_index_in_dim(weights_experts, expert_index, 0, keepdims=False)
    cot_rows = lax.dynamic_index_in_dim(cots_experts, expert_index, 0, keepdims=False)
    saved_state = expert_forward(recv_rows, gate_weight, up_weight, down_weight)
    return expert_backward(recv_rows, slot_weight, cot_rows, saved_state, gate_weight, up_weight, down_weight)


def unpack_block(back_rows, back_weight, target_slot):
    grouped = back_rows.reshape(EXPERTS, GROUP, CAP, D)
    expert_index = (target_slot // CAP).astype(jnp.int32)
    slot_index = (target_slot % CAP).astype(jnp.int32)
    picked = grouped[expert_index, :, slot_index].astype(jnp.float32).reshape(TOK_DEV, TOP, GROUP, D)
    token_rows = jnp.sum(picked, axis=(1, 2)).astype(jnp.bfloat16)
    weight_parts = back_weight.reshape(EXPERTS, GROUP, CAP)[expert_index, :, slot_index].astype(jnp.float32)
    route_rows = jnp.sum(weight_parts, axis=1).astype(jnp.bfloat16).reshape(TOK_DEV, TOP)
    return token_rows, route_rows


def to_experts(sent, trailing):
    return jnp.swapaxes(sent.reshape((N_EXPERT, EXPERTS, CAP) + trailing), 0, 1).reshape((EXPERTS, N_EXPERT * CAP) + trailing)


def to_sources(result, trailing):
    return jnp.swapaxes(result.reshape((N_EXPERT, N_EXPERT, CAP) + trailing), 0, 1)


def reference(tokens, expert_ids, route_weight, cotangent, w_gate, w_up, w_down):
    piece_expert = (jnp.arange(N_EXPERT, dtype=jnp.int32) // GROUP).astype(jnp.int32)
    term_list = []
    token_list = []
    route_list = []
    for section_index in range(N_PIPE):
        blocks = tokens[section_index].reshape(N_EXPERT, TOK_DEV, D)
        cot_blocks = cotangent[section_index].reshape(N_EXPERT, TOK_DEV, D)
        id_blocks = expert_ids[section_index].reshape(N_EXPERT, TOK_DEV, TOP)
        route_blocks = route_weight[section_index].reshape(N_EXPERT, TOK_DEV, TOP)
        source_row, target_slot = jax.vmap(partial(make_slots, experts=EXPERTS, capacity=CAP))(id_blocks)
        row_send = jax.vmap(partial(pack_rows, top_count=TOP))(source_row, blocks)
        cot_send = jax.vmap(partial(pack_rows, top_count=TOP))(source_row, cot_blocks)
        weight_send = jax.vmap(pack_weights)(source_row, route_blocks)
        gate_pieces = jnp.transpose(w_gate[section_index].reshape(D, N_EXPERT, HID_DEV), (1, 0, 2))
        up_pieces = jnp.transpose(w_up[section_index].reshape(D, N_EXPERT, HID_DEV), (1, 0, 2))
        down_pieces = w_down[section_index].reshape(N_EXPERT, HID_DEV, D)
        runner = partial(per_piece, rows_experts=to_experts(row_send, (D,)), weights_experts=to_experts(weight_send, ()), cots_experts=to_experts(cot_send, (D,)))
        outcome = lax.map(runner, (piece_expert, gate_pieces, up_pieces, down_pieces))
        row_grad, slot_grad, gate_term, up_term, down_term = outcome
        token_blocks, route_blocks_out = jax.vmap(unpack_block)(to_sources(row_grad, (D,)), to_sources(slot_grad, ()), target_slot)
        token_list.append(token_blocks.reshape(TOKENS, D))
        route_list.append(route_blocks_out.reshape(TOKENS, TOP))
        gate_full = jnp.transpose(gate_term, (1, 0, 2)).reshape(D, N_EXPERT * HID_DEV)
        up_full = jnp.transpose(up_term, (1, 0, 2)).reshape(D, N_EXPERT * HID_DEV)
        down_full = down_term.reshape(N_EXPERT * HID_DEV, D)
        term_list.append((gate_full, up_full, down_full))
    stacked = []
    for member in range(3):
        stacked.append(jnp.stack([(term_list[section_index][member].astype(jnp.float32) + term_list[section_index ^ 1][member].astype(jnp.float32)).astype(jnp.bfloat16) for section_index in range(N_PIPE)]))
    return jnp.stack(token_list), jnp.stack(route_list), stacked[0], stacked[1], stacked[2]
```

```python
import functools

import jax
import jax.numpy as jnp
import numpy as np
from jax import lax
from jax.experimental import pallas as pl
from jax.experimental.pallas import tpu as pltpu
from jax.sharding import PartitionSpec as P

MESH = pl.DeviceIdType.MESH
BF = jnp.bfloat16
F32 = jnp.float32
ROWS = 32
LANES = 128
FOLD = 16
SCALAR_ROW = 28
NY, NZ = 4, 8
GAIN_LIMIT = {(0, 0): 4, (0, 1): 3, (1, 0): 3, (1, 1): 4}


def dot(left, right):
    return jnp.dot(left, right, preferred_element_type=F32)


def dot_tn(left, right):
    return lax.dot_general(left, right, (((0,), (0,)), ((), ())), preferred_element_type=F32)


def dot_nt(left, right):
    return lax.dot_general(left, right, (((1,), (1,)), ((), ())), preferred_element_type=F32)


def fold_matrices(chunks):
    spread = np.zeros((chunks * FOLD, NZ * ROWS), np.float32)
    for chunk in range(chunks):
        for slot in range(NZ):
            spread[chunk * FOLD + slot, slot * ROWS + chunk] = 1.0
    place = np.zeros((NZ * ROWS, NZ * ROWS + FOLD), np.float32)
    for slot in range(NZ):
        place[slot * ROWS + SCALAR_ROW, slot * ROWS : (slot + 1) * ROWS] = 1.0
        place[slot * ROWS + SCALAR_ROW, NZ * ROWS + slot] = 1.0
    return jnp.asarray(spread, BF), jnp.asarray(spread.T, BF), jnp.asarray(place, BF)


def kernel(
    ids_col, ids_row, route, tokens, cot, w_gate, w_up, w_down, spread, spread_t, place,
    token_out, route_out, gu_out, down_out,
    ag, back, ring, stage, ret, acc, other, xq, cq, gu_w, gu_wt, down_wt, ov_rows, ov_grad, ov_hidden, stack, scaled,
    w_sem, y_send, y_recv, ag_send, ag_recv, rs_send, rs_recv, r_send, r_recv, p_send, p_recv,
):
    features = tokens.shape[1]
    chunks = features // LANES
    pairs = chunks // 2
    half = chunks // 2
    main = NZ * ROWS
    me_p = lax.axis_index("pipe")
    me_e = lax.axis_index("expert")
    y = lax.div(me_e, NZ)
    z = lax.rem(me_e, NZ)
    right = (me_p, y * NZ + lax.rem(z + 1, NZ))
    left = (me_p, y * NZ + lax.rem(z + NZ - 1, NZ))
    partner = (me_p + 1 - 2 * lax.rem(me_p, 2), me_e)
    ring_to = (right, left)

    def y_device(apart):
        return (me_p, lax.rem(y + apart, NY) * NZ + z)

    def weight_copies():
        return (
            pltpu.make_async_copy(w_gate, gu_w.at[:, 0:LANES], w_sem.at[0]),
            pltpu.make_async_copy(w_up, gu_w.at[:, LANES : 2 * LANES], w_sem.at[1]),
        )

    for copy in weight_copies():
        copy.start()

    barrier = pltpu.get_barrier_semaphore()
    for device in (right, left, y_device(1), y_device(2), y_device(3), partner):
        pl.semaphore_signal(barrier, inc=1, device_id=device, device_id_type=MESH)

    def y_copy(q, kind):
        return pltpu.make_async_remote_copy(
            src_ref=stage.at[q - 1, kind], dst_ref=ag.at[q, kind, 0],
            send_sem=y_send.at[q, kind], recv_sem=y_recv.at[q, kind],
            device_id=y_device(q), device_id_type=MESH,
        )

    def ag_copy(q, kind, way, hop):
        if way == 0:
            source, target = (NZ - hop + 1) % NZ, NZ - hop
        else:
            source, target = hop - 1, hop
        slot = kind * 2 + way
        return pltpu.make_async_remote_copy(
            src_ref=ag.at[q, kind, source], dst_ref=ag.at[q, kind, target],
            send_sem=ag_send.at[q, slot, hop - 1], recv_sem=ag_recv.at[q, slot, hop - 1],
            device_id=ring_to[way], device_id_type=MESH,
        )

    def part_of(part):
        return pl.ds(0, half) if part == 0 else pl.ds(half, chunks + 1 - half)

    def rs_slot(part, way, hop):
        hops = GAIN_LIMIT[(part, way)]
        return hops - hop if way == 0 else (NZ - hops + hop) % NZ

    def rs_copy(q, part, way, hop):
        slot = part * 2 + way
        extent = half if part == 0 else chunks + 1 - half
        return pltpu.make_async_remote_copy(
            src_ref=back.at[q, rs_slot(part, way, hop - 1), part_of(part)],
            dst_ref=ring.at[q, slot, hop - 1, pl.ds(0, extent)],
            send_sem=rs_send.at[q, slot, hop - 1], recv_sem=rs_recv.at[q, slot, hop - 1],
            device_id=ring_to[way], device_id_type=MESH,
        )

    def ret_copy(q):
        return pltpu.make_async_remote_copy(
            src_ref=back.at[q, 0], dst_ref=ret.at[q],
            send_sem=r_send.at[q], recv_sem=r_recv.at[q],
            device_id=y_device(NY - q), device_id_type=MESH,
        )

    def pair_copies():
        return (
            pltpu.make_async_remote_copy(
                src_ref=gu_out, dst_ref=other.at[0 : 2 * LANES], send_sem=p_send.at[0], recv_sem=p_recv.at[0],
                device_id=partner, device_id_type=MESH,
            ),
            pltpu.make_async_remote_copy(
                src_ref=down_out, dst_ref=other.at[2 * LANES : 3 * LANES], send_sem=p_send.at[1], recv_sem=p_recv.at[1],
                device_id=partner, device_id_type=MESH,
            ),
        )

    def codes():
        shift = y.astype(F32)
        col = ids_col[...].astype(F32) - shift
        col = jnp.where(col < 0, col + NY, col)
        row = ids_row[...].astype(F32) - shift
        row = jnp.where(row < 0, row + NY, row)
        count = col.shape[0]
        first = lax.broadcasted_iota(jnp.int32, (count, count), 0)
        second = lax.broadcasted_iota(jnp.int32, (count, count), 1)
        same = jnp.where(col == row, 1.0, 0.0)
        slot_row = jnp.sum(jnp.where(first < second, same, 0.0), axis=0, keepdims=True)
        slot_col = jnp.sum(jnp.where(second < first, same, 0.0), axis=1, keepdims=True)
        code_row = jnp.where(slot_row < ROWS, row * ROWS + slot_row, NY * ROWS + row)
        code_col = jnp.where(slot_col < ROWS, col * ROWS + slot_col, NY * ROWS + col)
        return col, slot_col, code_row, code_col

    def one_hot(code, shape, dim, start=0):
        places = lax.broadcasted_iota(jnp.int32, shape, dim) + start
        return jnp.where(places.astype(F32) == code, 1.0, 0.0).astype(BF)

    count = tokens.shape[0]
    _, _, code_row, _ = codes()
    pick = one_hot(code_row, (NY * ROWS + FOLD, count), 0)
    scaled[...] = (cot[...].astype(F32) * route[...].astype(F32)).astype(BF)
    for kind, values in ((0, tokens), (1, scaled)):
        for pair in range(pairs):
            rows = dot(pick, values[:, 2 * LANES * pair : 2 * LANES * (pair + 1)]).astype(BF)
            for side in range(2):
                chunk = 2 * pair + side
                part = rows[:, side * LANES : (side + 1) * LANES]
                ag[0, kind, 0, chunk] = part[0:ROWS]
                for q in range(1, NY):
                    stage[q - 1, kind, chunk] = part[q * ROWS : (q + 1) * ROWS]
                stack[chunk * FOLD : (chunk + 1) * FOLD] = part[NY * ROWS : NY * ROWS + FOLD]
        folded = dot(spread_t[0 : NY * ROWS], stack[...]).astype(BF)
        ag[0, kind, 0, chunks] = folded[0:ROWS]
        for q in range(1, NY):
            stage[q - 1, kind, chunks] = folded[q * ROWS : (q + 1) * ROWS]
        if kind == 0:
            pl.semaphore_wait(barrier, 6)
        for way in range(2):
            ag_copy(0, kind, way, 1).start()
        for q in range(1, NY):
            y_copy(q, kind).start()

    for copy in weight_copies():
        copy.wait()
    for chunk in range(chunks):
        span = slice(chunk * LANES, (chunk + 1) * LANES)
        gu_wt[:, span] = gu_w[span, :].T
        down_wt[span, :] = w_down[:, span].T
    acc[...] = jnp.zeros_like(acc)

    def gather_hop(q, hop):
        for kind in range(2):
            for way in range(2):
                if hop <= GAIN_LIMIT[(kind, way)]:
                    ag_copy(q, kind, way, hop).wait_recv()
                    if hop < GAIN_LIMIT[(kind, way)]:
                        ag_copy(q, kind, way, hop + 1).start()

    def reduce_start(q):
        for part in range(2):
            for way in range(2):
                rs_copy(q, part, way, 1).start()

    def reduce_hop(q, hop):
        for part in range(2):
            for way in range(2):
                hops = GAIN_LIMIT[(part, way)]
                if hop <= hops:
                    extent = half if part == 0 else chunks + 1 - half
                    rs_copy(q, part, way, hop).wait_recv()
                    target = back.at[q, rs_slot(part, way, hop), part_of(part)]
                    came = ring[q, part * 2 + way, hop - 1, 0:extent]
                    target[...] = (target[...].astype(F32) + came.astype(F32)).astype(BF)
                    if hop < hops:
                        rs_copy(q, part, way, hop + 1).start()

    def compute_rows(q):
        for kind, rows in ((0, xq), (1, cq)):
            folded = ag[q, kind, :, chunks].reshape(main, LANES)
            unfolded = dot(spread[...], folded).astype(BF)
            for chunk in range(chunks):
                span = slice(chunk * LANES, (chunk + 1) * LANES)
                rows[0:main, span] = ag[q, kind, :, chunk].reshape(main, LANES)
                extra = unfolded[chunk * FOLD : (chunk + 1) * FOLD]
                rows[main : main + FOLD, span] = extra
                ov_rows[kind, pl.ds(pl.multiple_of(q * FOLD, FOLD), FOLD), span] = extra
        pre = dot(xq[...], gu_w[...])
        gate, up = pre[:, 0:LANES], pre[:, LANES : 2 * LANES]
        hidden_grad = dot(cq[...], down_wt[...])
        sig = jax.nn.sigmoid(gate)
        hidden = (gate * sig * up).astype(BF)
        grad_gate = (hidden_grad * up * sig * (1.0 + gate * (1.0 - sig))).astype(BF)
        grad_up = (hidden_grad * gate * sig).astype(BF)
        grads = jnp.concatenate([grad_gate, grad_up], axis=1)
        mine = pl.ds(pl.multiple_of(q * FOLD, FOLD), FOLD)
        ov_grad[mine] = grads[main : main + FOLD]
        ov_hidden[mine] = hidden[main : main + FOLD]
        for pair in range(pairs):
            rows = dot(grads, gu_wt[:, 2 * LANES * pair : 2 * LANES * (pair + 1)]).astype(BF)
            for side in range(2):
                chunk = 2 * pair + side
                part = rows[:, side * LANES : (side + 1) * LANES]
                back[q, :, chunk] = part[0:main].reshape(NZ, ROWS, LANES)
                stack[chunk * FOLD : (chunk + 1) * FOLD] = part[main : main + FOLD]
        slot = jnp.sum(hidden.astype(F32) * hidden_grad, axis=1, keepdims=True)
        which = lax.broadcasted_iota(jnp.int32, (main + FOLD, LANES), 0)
        lane = lax.broadcasted_iota(jnp.int32, (main + FOLD, LANES), 1)
        wanted = jnp.where(which < main, lax.rem(which, ROWS), ROWS)
        spots = jnp.where(lane == wanted, slot, 0.0).astype(BF)
        folded = dot(spread_t[...], stack[...]) + dot(place[...], spots)
        back[q, :, chunks] = folded.astype(BF).reshape(NZ, ROWS, LANES)
        return grads[0:main], hidden[0:main]

    def compute_weights(grads, hidden):
        width = 4 * LANES
        for start in range(0, features, width):
            span = slice(start, start + width)
            acc[0 : 2 * LANES, span] += dot_tn(grads, xq[0:main, span])
            acc[2 * LANES : 3 * LANES, span] += dot_tn(hidden, cq[0:main, span])

    def next_quarter(q):
        for kind in range(2):
            y_copy(q, kind).wait_recv()
            for way in range(2):
                ag_copy(q, kind, way, 1).start()

    def finish_return(q):
        @pl.when(q > 0)
        def _():
            ret_copy(q).start()

    def quarter(q, carry):
        @pl.when(q == 0)
        def _():
            for hop in range(1, 5):
                gather_hop(q, hop)

        @pl.when(q > 0)
        def _():
            for hop in range(1, 5):
                gather_hop(q, hop)
                reduce_hop(q - 1, hop)
            finish_return(q - 1)

        @pl.when(q < NY - 1)
        def _():
            next_quarter(q + 1)

        grads, hidden = compute_rows(q)
        reduce_start(q)
        compute_weights(grads, hidden)
        return carry

    lax.fori_loop(0, NY, quarter, 0)

    width = 4 * LANES
    for start in range(0, features, width):
        span = slice(start, start + width)
        acc[0 : 2 * LANES, span] += dot_tn(ov_grad[...], ov_rows[0, :, span])
        acc[2 * LANES : 3 * LANES, span] += dot_tn(ov_hidden[...], ov_rows[1, :, span])
        gu_out[:, span] = acc[0 : 2 * LANES, span].astype(BF)
        down_out[:, span] = acc[2 * LANES : 3 * LANES, span].astype(BF)
    for copy in pair_copies():
        copy.start()

    for hop in range(1, 5):
        reduce_hop(NY - 1, hop)
    ret_copy(NY - 1).start()
    ret[0] = back[0, 0]

    for copy in pair_copies():
        copy.wait()
    for start in range(0, features, width):
        span = slice(start, start + width)
        gu_out[:, span] = (acc[0 : 2 * LANES, span] + other[0 : 2 * LANES, span].astype(F32)).astype(BF)
        down_out[:, span] = (acc[2 * LANES : 3 * LANES, span] + other[2 * LANES : 3 * LANES, span].astype(F32)).astype(BF)

    for q in range(1, NY):
        ret_copy(q).wait_recv()

    col, slot_col, _, code_col = codes()
    unpick = one_hot(code_col, (count, NY * ROWS), 1)
    unpick_fold = one_hot(code_col, (count, FOLD), 1, NY * ROWS)
    folded = ret[:, chunks].reshape(NY * ROWS, LANES)
    unfolded = dot(spread[:, 0 : NY * ROWS], folded).astype(BF)
    for chunk in range(chunks):
        rows = ret[:, chunk].reshape(NY * ROWS, LANES)
        total = dot(unpick, rows) + dot(unpick_fold, unfolded[chunk * FOLD : (chunk + 1) * FOLD])
        token_out[:, chunk * LANES : (chunk + 1) * LANES] = total.astype(BF)
    lane = lax.broadcasted_iota(jnp.int32, (count, LANES), 1).astype(F32)
    total = jnp.zeros((count, LANES), F32)
    for q in range(NY):
        entry = ret[q, chunks].astype(F32)[SCALAR_ROW : SCALAR_ROW + 1]
        total = total + jnp.where((lane == slot_col) & (col == q), entry, 0.0)
    slot_sum = jnp.sum(total, axis=1, keepdims=True)
    route_out[...] = (slot_sum / route[...].astype(F32)).astype(BF)

    for q in range(NY):
        for kind in range(2):
            if q > 0:
                y_copy(q, kind).wait_send()
            for way in range(2):
                for hop in range(1, GAIN_LIMIT[(kind, way)] + 1):
                    ag_copy(q, kind, way, hop).wait_send()
                    rs_copy(q, kind, way, hop).wait_send()
        if q > 0:
            ret_copy(q).wait_send()


def shards(tokens, expert_ids, route_weight, cotangent, w_gate, w_up, w_down):
    count, features = tokens.shape[1:]
    hidden = w_gate.shape[2]
    chunks = features // LANES
    spread, spread_t, place = fold_matrices(chunks)
    vmem = pl.BlockSpec(memory_space=pltpu.VMEM)
    anywhere = pl.BlockSpec(memory_space=pl.ANY)
    message = (chunks + 1, ROWS, LANES)
    larger = chunks + 1 - chunks // 2
    token_grad, route_grad, gu_grad, down_grad = pl.pallas_call(
        kernel,
        out_shape=(
            jax.ShapeDtypeStruct((count, features), BF),
            jax.ShapeDtypeStruct((count, 1), BF),
            jax.ShapeDtypeStruct((2 * hidden, features), BF),
            jax.ShapeDtypeStruct((hidden, features), BF),
        ),
        in_specs=[vmem] * 5 + [anywhere] * 2 + [vmem] * 4,
        out_specs=(vmem, vmem, vmem, vmem),
        scratch_shapes=[
            pltpu.VMEM((NY, 2, NZ) + message, BF),
            pltpu.VMEM((NY, NZ) + message, BF),
            pltpu.VMEM((NY, 4, 4, larger, ROWS, LANES), BF),
            pltpu.VMEM((NY - 1, 2) + message, BF),
            pltpu.VMEM((NY,) + message, BF),
            pltpu.VMEM((3 * hidden, features), F32),
            pltpu.VMEM((3 * hidden, features), BF),
            pltpu.VMEM((NZ * ROWS + FOLD, features), BF),
            pltpu.VMEM((NZ * ROWS + FOLD, features), BF),
            pltpu.VMEM((features, 2 * hidden), BF),
            pltpu.VMEM((2 * hidden, features), BF),
            pltpu.VMEM((features, hidden), BF),
            pltpu.VMEM((2, NY * FOLD, features), BF),
            pltpu.VMEM((NY * FOLD, 2 * hidden), BF),
            pltpu.VMEM((NY * FOLD, hidden), BF),
            pltpu.VMEM((chunks * FOLD, LANES), BF),
            pltpu.VMEM((count, features), BF),
            pltpu.SemaphoreType.DMA((2,)),
            pltpu.SemaphoreType.DMA((NY, 2)),
            pltpu.SemaphoreType.DMA((NY, 2)),
            pltpu.SemaphoreType.DMA((NY, 4, 4)),
            pltpu.SemaphoreType.DMA((NY, 4, 4)),
            pltpu.SemaphoreType.DMA((NY, 4, 4)),
            pltpu.SemaphoreType.DMA((NY, 4, 4)),
            pltpu.SemaphoreType.DMA((NY,)),
            pltpu.SemaphoreType.DMA((NY,)),
            pltpu.SemaphoreType.DMA((2,)),
            pltpu.SemaphoreType.DMA((2,)),
        ],
        compiler_params=pltpu.CompilerParams(
            collective_id=0, has_side_effects=True, vmem_limit_bytes=63 * 1024 * 1024
        ),
        cost_estimate=pl.CostEstimate(flops=8_000_000_000, bytes_accessed=10_000_000, transcendentals=140_000),
    )(
        expert_ids[0], expert_ids[0].reshape(1, count), route_weight[0], tokens[0], cotangent[0],
        w_gate[0], w_up[0], w_down[0], spread, spread_t, place,
    )
    grad_gate = gu_grad[0:hidden].T
    grad_up = gu_grad[hidden : 2 * hidden].T
    return (token_grad[None], route_grad[None], grad_gate[None], grad_up[None], down_grad[None])


def solution(mesh):
    rows = P("pipe", "expert", None)
    columns = P("pipe", None, "expert")
    return jax.shard_map(
        shards, mesh=mesh,
        in_specs=(rows, rows, rows, rows, columns, columns, rows),
        out_specs=(rows, rows, columns, columns, rows),
        check_vma=False,
    )
```

```python
import jax
import jax.numpy as jnp
import numpy as np
from jax import lax
from jax.experimental import pallas as pl
from jax.experimental.pallas import tpu as pltpu
from jax.sharding import PartitionSpec as P

MESH = pl.DeviceIdType.MESH
BF = jnp.bfloat16
F32 = jnp.float32
ROWS = 32
LANES = 128
FOLD = 16
HIGH, LOW = 28, 29
NY, NZ = 4, 8
HOPS = {(0, 0): 4, (0, 1): 3, (1, 0): 3, (1, 1): 4}


def dot(left, right):
    return jnp.dot(left, right, preferred_element_type=F32)


def dot_tn(left, right):
    return lax.dot_general(left, right, (((0,), (0,)), ((), ())), preferred_element_type=F32)


def dot_nt(left, right):
    return lax.dot_general(left, right, (((1,), (1,)), ((), ())), preferred_element_type=F32)


def fold_matrices(chunks):
    spread = np.zeros((chunks * FOLD, NZ * ROWS), np.float32)
    for chunk in range(chunks):
        for slot in range(NZ):
            spread[chunk * FOLD + slot, slot * ROWS + chunk] = 1.0
    place = np.zeros((2, NZ * ROWS, NZ * ROWS + FOLD), np.float32)
    for part, row in ((0, HIGH), (1, LOW)):
        for slot in range(NZ):
            place[part, slot * ROWS + row, slot * ROWS : (slot + 1) * ROWS] = 1.0
            place[part, slot * ROWS + row, NZ * ROWS + slot] = 1.0
    return jnp.asarray(spread, BF), jnp.asarray(spread.T, BF), jnp.asarray(place, BF)


def kernel(
    ids_row, route_row, tokens_in, cot_in, w_gate, w_up, w_down_in, spread, spread_t, place,
    token_out, route_out, gate_out, up_out, down_out,
    ag, back, ring, stage, ret, acc, other, xq, cq, gu_w, gu_wt, down_wt, ov_rows, ov_grad, ov_hidden, stack,
    w_sem, y_send, y_recv, ag_send, ag_recv, rs_send, rs_recv, r_send, r_recv, p_send, p_recv,
):
    count, features = tokens_in.shape
    tokens, cot, w_down = xq.at[0:count], xq.at[count : 2 * count], cq.at[0:count]
    own_gu = gu_wt
    scaled = cq.at[count : 2 * count]
    chunks = features // LANES
    pairs = chunks // 2
    half = chunks // 2
    main = NZ * ROWS
    me_p = lax.axis_index("pipe")
    me_e = lax.axis_index("expert")
    y = lax.div(me_e, NZ)
    z = lax.rem(me_e, NZ)
    right = (me_p, y * NZ + lax.rem(z + 1, NZ))
    left = (me_p, y * NZ + lax.rem(z + NZ - 1, NZ))
    partner = (me_p + 1 - 2 * lax.rem(me_p, 2), me_e)
    ring_to = (right, left)

    def y_device(apart):
        return (me_p, lax.rem(y + apart, NY) * NZ + z)

    def weight_copies():
        return (
            pltpu.make_async_copy(w_gate, gu_w.at[:, 0:LANES], w_sem.at[0]),
            pltpu.make_async_copy(w_up, gu_w.at[:, LANES : 2 * LANES], w_sem.at[1]),
            pltpu.make_async_copy(w_down_in, w_down, w_sem.at[2]),
        )

    loads = (
        pltpu.make_async_copy(tokens_in, tokens, w_sem.at[3]),
        pltpu.make_async_copy(cot_in, cot, w_sem.at[4]),
    )
    for copy in loads + weight_copies():
        copy.start()

    barrier = pltpu.get_barrier_semaphore()
    for device in (right, left, y_device(1), y_device(2), y_device(3), partner):
        pl.semaphore_signal(barrier, inc=1, device_id=device, device_id_type=MESH)

    def y_copy(q, kind):
        return pltpu.make_async_remote_copy(
            src_ref=stage.at[q - 1, kind], dst_ref=ag.at[q, kind, 0],
            send_sem=y_send.at[q, kind], recv_sem=y_recv.at[q, kind],
            device_id=y_device(q), device_id_type=MESH,
        )

    def ag_copy(q, kind, way, hop):
        if way == 0:
            source, target = (NZ - hop + 1) % NZ, NZ - hop
        else:
            source, target = hop - 1, hop
        slot = kind * 2 + way
        return pltpu.make_async_remote_copy(
            src_ref=ag.at[q, kind, source], dst_ref=ag.at[q, kind, target],
            send_sem=ag_send.at[q, slot, hop - 1], recv_sem=ag_recv.at[q, slot, hop - 1],
            device_id=ring_to[way], device_id_type=MESH,
        )

    def part_of(part):
        return pl.ds(0, half) if part == 0 else pl.ds(half, chunks + 1 - half)

    def rs_slot(part, way, hop):
        hops = HOPS[(part, way)]
        return hops - hop if way == 0 else (NZ - hops + hop) % NZ

    def rs_copy(q, part, way, hop):
        slot = part * 2 + way
        extent = half if part == 0 else chunks + 1 - half
        return pltpu.make_async_remote_copy(
            src_ref=back.at[q, rs_slot(part, way, hop - 1), part_of(part)],
            dst_ref=ring.at[q, slot, hop - 1, pl.ds(0, extent)],
            send_sem=rs_send.at[q, slot, hop - 1], recv_sem=rs_recv.at[q, slot, hop - 1],
            device_id=ring_to[way], device_id_type=MESH,
        )

    def ret_copy(q):
        return pltpu.make_async_remote_copy(
            src_ref=back.at[q, 0], dst_ref=ret.at[q],
            send_sem=r_send.at[q], recv_sem=r_recv.at[q],
            device_id=y_device(NY - q), device_id_type=MESH,
        )

    def pair_copies():
        return (
            pltpu.make_async_remote_copy(
                src_ref=own_gu, dst_ref=other.at[0 : 2 * LANES], send_sem=p_send.at[0], recv_sem=p_recv.at[0],
                device_id=partner, device_id_type=MESH,
            ),
            pltpu.make_async_remote_copy(
                src_ref=down_out, dst_ref=other.at[2 * LANES : 3 * LANES], send_sem=p_send.at[1], recv_sem=p_recv.at[1],
                device_id=partner, device_id_type=MESH,
            ),
        )

    def to_column(row):
        first = lax.broadcasted_iota(jnp.int32, (count, count), 0)
        second = lax.broadcasted_iota(jnp.int32, (count, count), 1)
        return jnp.sum(jnp.where(first == second, row, 0.0), axis=1, keepdims=True)

    def codes():
        rel = ids_row[...].astype(F32) - y.astype(F32)
        row = jnp.where(rel < 0, rel + NY, rel)
        col = to_column(row)
        first = lax.broadcasted_iota(jnp.int32, (count, count), 0)
        second = lax.broadcasted_iota(jnp.int32, (count, count), 1)
        same = jnp.where(col == row, 1.0, 0.0)
        slot_row = jnp.sum(jnp.where(first < second, same, 0.0), axis=0, keepdims=True)
        slot_col = jnp.sum(jnp.where(second < first, same, 0.0), axis=1, keepdims=True)
        code_row = jnp.where(slot_row < ROWS, row * ROWS + slot_row, NY * ROWS + row)
        code_col = jnp.where(slot_col < ROWS, col * ROWS + slot_col, NY * ROWS + col)
        return col, slot_col, code_row, code_col

    def one_hot(code, shape, dim, start=0):
        places = lax.broadcasted_iota(jnp.int32, shape, dim) + start
        return jnp.where(places.astype(F32) == code, 1.0, 0.0).astype(BF)

    _, _, code_row, _ = codes()
    pick = one_hot(code_row, (NY * ROWS + FOLD, count), 0)
    loads[0].wait()
    for kind, values in ((0, tokens), (1, scaled)):
        if kind == 1:
            loads[1].wait()
            scaled[...] = (cot[...].astype(F32) * to_column(route_row[...].astype(F32))).astype(BF)
        for pair in range(pairs):
            rows = dot(pick, values[:, 2 * LANES * pair : 2 * LANES * (pair + 1)]).astype(BF)
            for side in range(2):
                chunk = 2 * pair + side
                part = rows[:, side * LANES : (side + 1) * LANES]
                ag[0, kind, 0, chunk] = part[0:ROWS]
                for q in range(1, NY):
                    stage[q - 1, kind, chunk] = part[q * ROWS : (q + 1) * ROWS]
                stack[chunk * FOLD : (chunk + 1) * FOLD] = part[NY * ROWS : NY * ROWS + FOLD]
        folded = dot(spread_t[0 : NY * ROWS], stack[...]).astype(BF)
        ag[0, kind, 0, chunks] = folded[0:ROWS]
        for q in range(1, NY):
            stage[q - 1, kind, chunks] = folded[q * ROWS : (q + 1) * ROWS]
        if kind == 0:
            pl.semaphore_wait(barrier, 6)
        for way in range(2):
            ag_copy(0, kind, way, 1).start()
        for q in range(1, NY):
            y_copy(q, kind).start()

    for copy in weight_copies():
        copy.wait()
    for chunk in range(chunks):
        span = slice(chunk * LANES, (chunk + 1) * LANES)
        gu_wt[:, span] = gu_w[span, :].T
        down_wt[span, :] = w_down[:, span].T
    acc[...] = jnp.zeros_like(acc)

    def gather_hop(q, hop):
        for kind in range(2):
            for way in range(2):
                if hop <= HOPS[(kind, way)]:
                    ag_copy(q, kind, way, hop).wait_recv()
                    if hop < HOPS[(kind, way)]:
                        ag_copy(q, kind, way, hop + 1).start()

    def reduce_start(q):
        for part in range(2):
            for way in range(2):
                rs_copy(q, part, way, 1).start()

    def merge(first, second):
        total = first.astype(F32) + second.astype(F32)
        sums = total[HIGH : HIGH + 1] + total[LOW : LOW + 1]
        high = sums.astype(BF).astype(F32)
        row = lax.broadcasted_iota(jnp.int32, (ROWS, LANES), 0)
        return jnp.where(row == HIGH, high, jnp.where(row == LOW, sums - high, total)).astype(BF)

    def reduce_hop(q, hop):
        for part in range(2):
            for way in range(2):
                hops = HOPS[(part, way)]
                if hop <= hops:
                    rs_copy(q, part, way, hop).wait_recv()
                    target = back.at[q, rs_slot(part, way, hop), part_of(part)]
                    came = ring.at[q, part * 2 + way, hop - 1]
                    target[0:half] = (target[0:half].astype(F32) + came[0:half].astype(F32)).astype(BF)
                    if part == 1:
                        target[half] = merge(target[half], came[half])
                    if hop < hops:
                        rs_copy(q, part, way, hop + 1).start()

    def compute_rows(q):
        for kind, rows in ((0, xq), (1, cq)):
            folded = ag[q, kind, :, chunks].reshape(main, LANES)
            unfolded = dot(spread[...], folded).astype(BF)
            for chunk in range(chunks):
                span = slice(chunk * LANES, (chunk + 1) * LANES)
                rows[0:main, span] = ag[q, kind, :, chunk].reshape(main, LANES)
                extra = unfolded[chunk * FOLD : (chunk + 1) * FOLD]
                rows[main : main + FOLD, span] = extra
                ov_rows[kind, pl.ds(pl.multiple_of(q * FOLD, FOLD), FOLD), span] = extra
        pre = dot(xq[...], gu_w[...])
        gate, up = pre[:, 0:LANES], pre[:, LANES : 2 * LANES]
        hidden_grad = dot(cq[...], down_wt[...])
        sig = jax.nn.sigmoid(gate)
        hidden = (gate * sig * up).astype(BF)
        grad_gate = (hidden_grad * up * sig * (1.0 + gate * (1.0 - sig))).astype(BF)
        grad_up = (hidden_grad * gate * sig).astype(BF)
        grads = jnp.concatenate([grad_gate, grad_up], axis=1)
        mine = pl.ds(pl.multiple_of(q * FOLD, FOLD), FOLD)
        ov_grad[mine] = grads[main : main + FOLD]
        ov_hidden[mine] = hidden[main : main + FOLD]
        for pair in range(pairs):
            rows = dot(grads, gu_wt[:, 2 * LANES * pair : 2 * LANES * (pair + 1)]).astype(BF)
            for side in range(2):
                chunk = 2 * pair + side
                part = rows[:, side * LANES : (side + 1) * LANES]
                back[q, :, chunk] = part[0:main].reshape(NZ, ROWS, LANES)
                stack[chunk * FOLD : (chunk + 1) * FOLD] = part[main : main + FOLD]
        slot = jnp.sum(hidden.astype(F32) * hidden_grad, axis=1, keepdims=True)
        which = lax.broadcasted_iota(jnp.int32, (main + FOLD, LANES), 0)
        lane = lax.broadcasted_iota(jnp.int32, (main + FOLD, LANES), 1)
        wanted = jnp.where(which < main, lax.rem(which, ROWS), ROWS)
        spots = jnp.where(lane == wanted, slot, 0.0)
        high = spots.astype(BF)
        low = (spots - high.astype(F32)).astype(BF)
        folded = dot(spread_t[...], stack[...]) + dot(place[0], high) + dot(place[1], low)
        back[q, :, chunks] = folded.astype(BF).reshape(NZ, ROWS, LANES)
        return grads[0:main], hidden[0:main]

    def compute_weights(grads, hidden):
        width = 4 * LANES
        for start in range(0, features, width):
            span = slice(start, start + width)
            acc[0 : 2 * LANES, span] += dot_tn(grads, xq[0:main, span])
            acc[2 * LANES : 3 * LANES, span] += dot_tn(hidden, cq[0:main, span])

    def next_quarter(q):
        for kind in range(2):
            y_copy(q, kind).wait_recv()
            for way in range(2):
                ag_copy(q, kind, way, 1).start()

    def quarter(q, carry):
        gather_hop(q, 3)

        @pl.when(q >= 2)
        def _():
            reduce_hop(q - 1, 1)

        gather_hop(q, 4)

        @pl.when(q >= 2)
        def _():
            reduce_hop(q - 1, 2)

        @pl.when(q < NY - 1)
        def _():
            gather_hop(q + 1, 1)

        grads, hidden = compute_rows(q)
        reduce_start(q)

        @pl.when(q < NY - 2)
        def _():
            next_quarter(q + 2)

        @pl.when(q == 2)
        def _():
            reduce_hop(q - 1, 3)

        @pl.when(q < NY - 1)
        def _():
            gather_hop(q + 1, 2)

        @pl.when(q == 2)
        def _():
            reduce_hop(q - 1, 4)
            ret_copy(q - 1).start()

        compute_weights(grads, hidden)
        return carry

    gather_hop(0, 1)
    next_quarter(1)
    gather_hop(0, 2)
    lax.fori_loop(0, NY, quarter, 0)
    reduce_hop(2, 3)

    width = 4 * LANES
    for start in range(0, features, width):
        span = slice(start, start + width)
        acc[0 : 2 * LANES, span] += dot_tn(ov_grad[...], ov_rows[0, :, span])
        acc[2 * LANES : 3 * LANES, span] += dot_tn(ov_hidden[...], ov_rows[1, :, span])
        own_gu[:, span] = acc[0 : 2 * LANES, span].astype(BF)
        down_out[:, span] = acc[2 * LANES : 3 * LANES, span].astype(BF)
    for copy in pair_copies():
        copy.start()

    reduce_hop(3, 1)
    reduce_hop(0, 1)
    reduce_hop(2, 4)
    ret_copy(2).start()
    for hop in range(2, 5):
        reduce_hop(3, hop)
        if hop == 4:
            ret_copy(3).start()
        reduce_hop(0, hop)
    ret[0] = back[0, 0]

    for copy in pair_copies():
        copy.wait()
    for start in range(0, features, width):
        span = slice(start, start + width)
        both = (acc[0 : 2 * LANES, span] + other[0 : 2 * LANES, span].astype(F32)).astype(BF)
        for part in range(0, width, LANES):
            here = slice(start + part, start + part + LANES)
            gate_out[here] = both[0:LANES, part : part + LANES].T
            up_out[here] = both[LANES : 2 * LANES, part : part + LANES].T
        down_out[:, span] = (acc[2 * LANES : 3 * LANES, span] + other[2 * LANES : 3 * LANES, span].astype(F32)).astype(BF)

    for q in range(1, NY):
        ret_copy(q).wait_recv()

    col, slot_col, _, code_col = codes()
    unpick = one_hot(code_col, (count, NY * ROWS), 1)
    unpick_fold = one_hot(code_col, (count, FOLD), 1, NY * ROWS)
    folded = ret[:, chunks].reshape(NY * ROWS, LANES)
    unfolded = dot(spread[:, 0 : NY * ROWS], folded).astype(BF)
    for chunk in range(chunks):
        rows = ret[:, chunk].reshape(NY * ROWS, LANES)
        total = dot(unpick, rows) + dot(unpick_fold, unfolded[chunk * FOLD : (chunk + 1) * FOLD])
        token_out[:, chunk * LANES : (chunk + 1) * LANES] = total.astype(BF)
    lane = lax.broadcasted_iota(jnp.int32, (count, LANES), 1).astype(F32)
    total = jnp.zeros((count, LANES), F32)
    for q in range(NY):
        last = ret[q, chunks].astype(F32)
        entry = last[HIGH : HIGH + 1] + last[LOW : LOW + 1]
        total = total + jnp.where((lane == slot_col) & (col == q), entry, 0.0)
    slot_sum = jnp.sum(total, axis=1, keepdims=True)
    first = lax.broadcasted_iota(jnp.int32, (count, count), 0)
    second = lax.broadcasted_iota(jnp.int32, (count, count), 1)
    sum_row = jnp.sum(jnp.where(first == second, slot_sum, 0.0), axis=0, keepdims=True)
    route_out[...] = (sum_row / route_row[...].astype(F32)).astype(BF)

    for q in range(NY):
        for kind in range(2):
            if q > 0:
                y_copy(q, kind).wait_send()
            for way in range(2):
                for hop in range(1, HOPS[(kind, way)] + 1):
                    ag_copy(q, kind, way, hop).wait_send()
                    rs_copy(q, kind, way, hop).wait_send()
        if q > 0:
            ret_copy(q).wait_send()


def shards(tokens, expert_ids, route_weight, cotangent, w_gate, w_up, w_down):
    count, features = tokens.shape[1:]
    hidden = w_gate.shape[2]
    chunks = features // LANES
    spread, spread_t, place = fold_matrices(chunks)
    vmem = pl.BlockSpec(memory_space=pltpu.VMEM)
    anywhere = pl.BlockSpec(memory_space=pl.ANY)
    message = (chunks + 1, ROWS, LANES)
    larger = chunks + 1 - chunks // 2
    token_grad, route_grad, gate_grad, up_grad, down_grad = pl.pallas_call(
        kernel,
        out_shape=(
            jax.ShapeDtypeStruct((count, features), BF),
            jax.ShapeDtypeStruct((1, count), BF),
            jax.ShapeDtypeStruct((features, hidden), BF),
            jax.ShapeDtypeStruct((features, hidden), BF),
            jax.ShapeDtypeStruct((hidden, features), BF),
        ),
        in_specs=[vmem] * 2 + [anywhere] * 5 + [vmem] * 3,
        out_specs=(vmem,) * 5,
        scratch_shapes=[
            pltpu.VMEM((NY, 2, NZ) + message, BF),
            pltpu.VMEM((NY, NZ) + message, BF),
            pltpu.VMEM((NY, 4, 4, larger, ROWS, LANES), BF),
            pltpu.VMEM((NY - 1, 2) + message, BF),
            pltpu.VMEM((NY,) + message, BF),
            pltpu.VMEM((3 * hidden, features), F32),
            pltpu.VMEM((3 * hidden, features), BF),
            pltpu.VMEM((NZ * ROWS + FOLD, features), BF),
            pltpu.VMEM((NZ * ROWS + FOLD, features), BF),
            pltpu.VMEM((features, 2 * hidden), BF),
            pltpu.VMEM((2 * hidden, features), BF),
            pltpu.VMEM((features, hidden), BF),
            pltpu.VMEM((2, NY * FOLD, features), BF),
            pltpu.VMEM((NY * FOLD, 2 * hidden), BF),
            pltpu.VMEM((NY * FOLD, hidden), BF),
            pltpu.VMEM((chunks * FOLD, LANES), BF),
            pltpu.SemaphoreType.DMA((5,)),
            pltpu.SemaphoreType.DMA((NY, 2)),
            pltpu.SemaphoreType.DMA((NY, 2)),
            pltpu.SemaphoreType.DMA((NY, 4, 4)),
            pltpu.SemaphoreType.DMA((NY, 4, 4)),
            pltpu.SemaphoreType.DMA((NY, 4, 4)),
            pltpu.SemaphoreType.DMA((NY, 4, 4)),
            pltpu.SemaphoreType.DMA((NY,)),
            pltpu.SemaphoreType.DMA((NY,)),
            pltpu.SemaphoreType.DMA((2,)),
            pltpu.SemaphoreType.DMA((2,)),
        ],
        compiler_params=pltpu.CompilerParams(
            collective_id=0, has_side_effects=True, vmem_limit_bytes=63 * 1024 * 1024
        ),
        cost_estimate=pl.CostEstimate(flops=8_000_000_000, bytes_accessed=10_000_000, transcendentals=140_000),
    )(
        expert_ids.reshape(1, count), route_weight.reshape(1, count), tokens[0], cotangent[0],
        w_gate[0], w_up[0], w_down[0], spread, spread_t, place,
    )
    return (token_grad[None], route_grad.reshape(1, count, 1), gate_grad[None], up_grad[None], down_grad[None])


def solution(mesh):
    rows = P("pipe", "expert", None)
    columns = P("pipe", None, "expert")
    return jax.shard_map(
        shards, mesh=mesh,
        in_specs=(rows, rows, rows, rows, columns, columns, rows),
        out_specs=(rows, rows, columns, columns, rows),
        check_vma=False,
    )
```

```python
import jax
import jax.numpy as jnp
import numpy as np
from jax import lax
from jax.experimental import pallas as pl
from jax.experimental.pallas import tpu as pltpu
from jax.sharding import PartitionSpec as P

MESH = pl.DeviceIdType.MESH
BF = jnp.bfloat16
F32 = jnp.float32
ROWS = 32
LANES = 128
FOLD = 16
HIGH, LOW = 28, 29
NY, NZ, LINE = 4, 8, 4
MAIN = LINE * ROWS
QROWS = MAIN + FOLD


def dot(left, right):
    return jnp.dot(left, right, preferred_element_type=F32)


def fold_matrices(chunks):
    spread = np.zeros((chunks * FOLD, MAIN), np.float32)
    for chunk in range(chunks):
        for slot in range(LINE):
            spread[chunk * FOLD + slot, slot * ROWS + chunk] = 1.0
    place = np.zeros((2, MAIN, QROWS), np.float32)
    for part, row in ((0, HIGH), (1, LOW)):
        for slot in range(LINE):
            place[part, slot * ROWS + row, slot * ROWS : (slot + 1) * ROWS] = 1.0
            place[part, slot * ROWS + row, MAIN + slot] = 1.0
    return jnp.asarray(spread, BF), jnp.asarray(spread.T, BF), jnp.asarray(place, BF)


def kernel(
    ids_row, route_row, tokens_in, cot_in, w_gate, w_up, w_down_in, spread, spread_t, place,
    token_out, route_out, grad_out,
    buf, back, ring, relay, back_relay, ret, w_nat, gu_wt, x_all, c_all, grads_all, grads_t, relay_in, relay_on,
    mirror_half, own_half, far_half, grad_in, grad_on, stack,
    w_sem, ag_send, ag_recv, y_send, y_recv, relay_send, relay_recv, r_send, r_recv, rs_send, rs_recv,
    m_send, m_recv, d_send, d_recv, c_send, c_recv,
):
    count, features = tokens_in.shape
    tokens, cot, w_down = (x_all.at[index * count : (index + 1) * count] for index in range(3))
    mirror_grad, own_grad = grad_out, gu_wt.at[0 : 3 * LANES]
    chunks = features // LANES
    pairs = chunks // 2
    half = features // 2
    direct = half // 2
    pieces = tuple((start, min(2 * LANES, half - start)) for start in range(direct, half, 2 * LANES))
    me_p = lax.axis_index("pipe")
    me_e = lax.axis_index("expert")
    plane = lax.div(me_p, 2)
    core = lax.rem(me_p, 2)
    y = lax.div(me_e, NZ)
    z = lax.rem(me_e, NZ)
    turn = lax.rem(y + 2 * plane, LINE)
    right = (me_p, y * NZ + lax.rem(z + 1, NZ))
    left = (me_p, y * NZ + lax.rem(z + NZ - 1, NZ))
    partner = (me_p + 1 - 2 * core, me_e)
    planes = lax.axis_size("pipe") // 2
    beside = tuple((2 * lax.rem(plane + apart, planes) + core, me_e) for apart in (1, planes - 1))
    mirror = (me_p, y * NZ + lax.rem(2 * turn + 7 - z + NZ, NZ))
    mirror_on = (me_p, y * NZ + lax.rem(2 * lax.rem(turn + 2, LINE) + 7 - z + NZ, NZ))
    ring_to = (right, left)
    base = core * half
    away = half - base

    def y_device(apart):
        return (me_p, lax.rem(y + apart, NY) * NZ + z)

    def position(q):
        return lax.rem(z + LINE - lax.rem(turn + q, LINE), LINE)

    def landed(q):
        return q + 3 - 3 * lax.div(3 - q, 3)

    def remote(source, target, send, recv, device):
        return pltpu.make_async_remote_copy(
            src_ref=source, dst_ref=target, send_sem=send, recv_sem=recv, device_id=device, device_id_type=MESH
        )

    def ag_copy(q, kind, way, slot):
        at = buf.at[q, kind, slot]
        return remote(at, at, ag_send.at[q, kind, way, slot], ag_recv.at[q, kind, slot], ring_to[way])

    def y_copy(q, kind, slot):
        return remote(buf.at[q, kind, slot], buf.at[q + 3, kind, slot], y_send.at[q, kind, slot], y_recv.at[q, kind, slot], y_device(q))

    def y_half(kind, slot):
        return remote(buf.at[2, kind, slot], relay.at[kind, slot], y_send.at[2, kind, slot], relay_recv.at[kind, slot], y_device(1 + 2 * kind))

    def y_rest(kind, slot):
        return remote(relay.at[kind, slot], buf.at[5, kind, slot], relay_send.at[kind, slot], y_recv.at[2, kind, slot], y_device(1 + 2 * kind))

    def r_half(slot):
        return remote(back.at[5, slot], back_relay.at[slot], r_send.at[2, slot], relay_recv.at[2, slot], y_device(1 + slot // 2 * 2))

    def r_rest(slot):
        return remote(back_relay.at[slot], back.at[2, slot], relay_send.at[2, slot], r_recv.at[2, slot], y_device(1 + slot // 2 * 2))

    def y_start(q, kind, slot):
        if q == 2:
            y_half(kind, slot).start()
        elif q > 0:
            y_copy(q, kind, slot).start()

    def relay_hop(hop):
        for kind in range(2):
            place_at = position(1 + 2 * kind)

            def onward(slot):
                y_half(kind, slot).wait_recv()
                y_rest(kind, slot).start()

            if hop == 0:
                onward(place_at)
                continue

            @pl.when(place_at >= hop)
            def _():
                onward(place_at - hop)

            @pl.when(place_at + hop < LINE)
            def _():
                onward(place_at + hop)

    def r_copy(q, slot):
        return remote(back.at[q + 3, slot], back.at[q, slot], r_send.at[q, slot], r_recv.at[q, slot], y_device(NY - q))

    def rs_copy(q, way, slot):
        return remote(back.at[q, slot], ring.at[q, way, slot - 1 + way], rs_send.at[q, way, slot], rs_recv.at[q, way, slot], ring_to[way])

    def rows_at(offset, size):
        return pl.ds(pl.multiple_of(base + offset, LANES), size)

    def weight_copy(leg, piece):
        if leg == 0:
            span = rows_at(0, direct)
            return remote(w_nat.at[0, span], w_nat.at[1, span], m_send.at[0], m_recv.at[0], mirror)
        offset, size = pieces[piece]
        span, local = rows_at(offset, size), pl.ds(offset - direct, size)
        number = len(pieces) * (leg - 1) + 1 + piece
        there, back_there = beside[piece % 2], beside[1 - piece % 2]
        if leg == 1:
            return remote(w_nat.at[0, span], relay_in.at[local], m_send.at[number], m_recv.at[number], there)
        if leg == 2:
            return remote(relay_in.at[local], relay_on.at[local], m_send.at[number], m_recv.at[number], mirror_on)
        return remote(relay_on.at[local], w_nat.at[1, span], m_send.at[number], m_recv.at[number], back_there)

    def grad_copy(leg, piece):
        if leg == 0:
            return remote(mirror_grad.at[:, rows_at(0, direct)], far_half.at[:, 0:direct], d_send.at[0], d_recv.at[0], mirror)
        offset, size = pieces[piece]
        span, local = rows_at(offset, size), pl.ds(offset - direct, size)
        number = len(pieces) * (leg - 1) + 1 + piece
        there, back_there = beside[piece % 2], beside[1 - piece % 2]
        if leg == 1:
            return remote(mirror_grad.at[:, span], grad_in.at[:, local], d_send.at[number], d_recv.at[number], there)
        if leg == 2:
            return remote(grad_in.at[:, local], grad_on.at[:, local], d_send.at[number], d_recv.at[number], mirror_on)
        return remote(grad_on.at[:, local], far_half.at[:, offset : offset + size], d_send.at[number], d_recv.at[number], back_there)

    def core_copy(number):
        if number < 2:
            span = rows_at(number * direct, direct)
            return remote(w_nat.at[1, span], w_nat.at[1, span], c_send.at[number], c_recv.at[number], partner)
        mine, other = rows_at(0, half), pl.ds(pl.multiple_of(away, LANES), half)
        if number == 2:
            return remote(mirror_grad.at[:, other], mirror_half, c_send.at[2], c_recv.at[2], partner)
        if number == 3:
            return remote(gu_wt.at[0 : 3 * LANES, other], own_half, c_send.at[3], c_recv.at[3], partner)
        return remote(grad_out.at[:, mine], grad_out.at[:, mine], c_send.at[4], c_recv.at[4], partner)

    def codes():
        rel = ids_row[...].astype(F32) - y.astype(F32)
        row = jnp.where(rel < 0, rel + NY, rel)
        first = lax.broadcasted_iota(jnp.int32, (count, count), 0)
        second = lax.broadcasted_iota(jnp.int32, (count, count), 1)
        col = to_column(row)
        same = jnp.where(col == row, 1.0, 0.0)
        slot_row = jnp.sum(jnp.where(first < second, same, 0.0), axis=0, keepdims=True)
        slot_col = jnp.sum(jnp.where(second < first, same, 0.0), axis=1, keepdims=True)
        code_row = jnp.where(slot_row < ROWS, row * ROWS + slot_row, MAIN + row)
        code_col = jnp.where(slot_col < ROWS, col * ROWS + slot_col, MAIN + col)
        return col, slot_col, code_row, code_col

    def to_column(row):
        first = lax.broadcasted_iota(jnp.int32, (count, count), 0)
        second = lax.broadcasted_iota(jnp.int32, (count, count), 1)
        return jnp.sum(jnp.where(first == second, row, 0.0), axis=1, keepdims=True)

    def one_hot(code, shape, dim, start=0):
        places = lax.broadcasted_iota(jnp.int32, shape, dim) + start
        return jnp.where(places.astype(F32) == code, 1.0, 0.0).astype(BF)

    def transposed(piece):
        for chunk in range(chunks):
            span = slice(chunk * LANES, (chunk + 1) * LANES)
            gu_wt[2 * LANES * piece : 2 * LANES * (piece + 1), span] = w_nat[piece, span, 0 : 2 * LANES].T

    loads = (
        pltpu.make_async_copy(w_gate, w_nat.at[0, :, 0:LANES], w_sem.at[0]),
        pltpu.make_async_copy(w_up, w_nat.at[0, :, LANES : 2 * LANES], w_sem.at[1]),
        pltpu.make_async_copy(w_down_in, w_down, w_sem.at[2]),
        pltpu.make_async_copy(tokens_in, tokens, w_sem.at[3]),
        pltpu.make_async_copy(cot_in, cot, w_sem.at[4]),
    )
    for copy in loads:
        copy.start()
    barrier = pltpu.get_barrier_semaphore()
    for device in (right, left, y_device(1), y_device(2), y_device(3), partner) + beside + (mirror, mirror_on):
        pl.semaphore_signal(barrier, inc=1, device_id=device, device_id_type=MESH)
    loads[2].wait()
    for chunk in range(chunks):
        span = slice(chunk * LANES, (chunk + 1) * LANES)
        w_nat[0, span, 2 * LANES : 3 * LANES] = w_down[:, span].T
    for index in (0, 1, 3, 4):
        loads[index].wait()
    pl.semaphore_wait(barrier, 10)
    for piece in range(len(pieces)):
        weight_copy(1, piece).start()
    weight_copy(0, 0).start()

    def own_start(q, kind):
        place_at = position(q)

        @pl.when(place_at < LINE - 1)
        def _():
            ag_copy(q, kind, 0, place_at).start()

        @pl.when(place_at > 0)
        def _():
            ag_copy(q, kind, 1, place_at).start()

        y_start(q, kind, place_at)

    _, _, code_row, _ = codes()
    pick = one_hot(code_row, (QROWS, count), 0)
    c_all[0:count] = (cot[...].astype(F32) * to_column(route_row[...].astype(F32))).astype(BF)
    for kind, values in ((0, tokens), (1, c_all)):
        for pair in range(pairs):
            rows = dot(pick, values[0:count, 2 * LANES * pair : 2 * LANES * (pair + 1)]).astype(BF)
            for side in range(2):
                chunk = 2 * pair + side
                part = rows[:, side * LANES : (side + 1) * LANES]
                for q in range(NY):
                    buf[q, kind, position(q), chunk] = part[q * ROWS : (q + 1) * ROWS]
                stack[chunk * FOLD : (chunk + 1) * FOLD] = part[MAIN:QROWS]
        folded = dot(spread_t[...], stack[...]).astype(BF)
        for q in range(NY):
            buf[q, kind, position(q), chunks] = folded[q * ROWS : (q + 1) * ROWS]
        for q in (2, 1, 3, 0):
            own_start(q, kind)

    def gather_hop(q, hop):
        place_at = position(q)

        def one_kind(kind, carry):
            def arrived(way, slot, onward):
                ag_copy(q, kind, way, slot).wait_recv()

                @pl.when(onward)
                def _():
                    ag_copy(q, kind, way, slot).start()

                y_start(q, kind, slot)

            @pl.when(place_at >= hop)
            def _():
                arrived(0, place_at - hop, place_at < LINE - 1)

            @pl.when(place_at + hop < LINE)
            def _():
                arrived(1, place_at + hop, place_at > 0)

            return carry

        lax.fori_loop(0, 2, one_kind, 0)

    def merge(first, second):
        total = first.astype(F32) + second.astype(F32)
        sums = total[HIGH : HIGH + 1] + total[LOW : LOW + 1]
        high = sums.astype(BF).astype(F32)
        row = lax.broadcasted_iota(jnp.int32, (ROWS, LANES), 0)
        return jnp.where(row == HIGH, high, jnp.where(row == LOW, sums - high, total)).astype(BF)

    def add_message(target, first, second):
        target[0:chunks] = (first[0:chunks].astype(F32) + second[0:chunks].astype(F32)).astype(BF)
        target[chunks] = merge(first[chunks], second[chunks])

    def reduce_level(q, level):
        place_at = position(q)

        def step(way, slot, came):
            if level > 0:
                rs_copy(q, way, slot).wait_recv()
                add_message(back.at[q, slot], back.at[q, slot], ring.at[q, way, came])
            rs_copy(q, way, slot).start()

        @pl.when(place_at == level)
        def _():
            for slot in range(LINE - 1, level, -1):
                step(0, slot, slot - 1)

        @pl.when(place_at == LINE - 1 - level)
        def _():
            for slot in range(LINE - 1 - level):
                step(1, slot, slot)

    def reduce_end(q):
        place_at = position(q)
        ret[q] = back[q, place_at]

        @pl.when(place_at > 0)
        def _():
            rs_copy(q, 0, place_at).wait_recv()
            add_message(ret.at[q], ret.at[q], ring.at[q, 0, place_at - 1])

        @pl.when(place_at < LINE - 1)
        def _():
            rs_copy(q, 1, place_at).wait_recv()
            add_message(ret.at[q], ret.at[q], ring.at[q, 1, place_at])

    def returned(q):
        for slot in range(LINE):
            r_copy(q, slot).wait_recv()

    def compute_rows(q):
        at = landed(q)
        start = q * QROWS
        block = pl.ds(pl.multiple_of(start, FOLD), QROWS)
        for kind, rows in ((0, x_all), (1, c_all)):
            folded = buf[at, kind, :, chunks].reshape(MAIN, LANES)
            unfolded = dot(spread[...], folded).astype(BF)
            for chunk in range(chunks):
                span = slice(chunk * LANES, (chunk + 1) * LANES)
                rows[pl.ds(pl.multiple_of(start, FOLD), MAIN), span] = buf[at, kind, :, chunk].reshape(MAIN, LANES)
                rows[pl.ds(pl.multiple_of(start + MAIN, FOLD), FOLD), span] = unfolded[chunk * FOLD : (chunk + 1) * FOLD]
        slot = jnp.zeros((QROWS, 1), F32)
        both = []
        for piece in range(2):
            pre = dot(x_all[block], w_nat[piece, :, 0 : 2 * LANES])
            gate, up = pre[:, 0:LANES], pre[:, LANES : 2 * LANES]
            hidden_grad = dot(c_all[block], w_nat[piece, :, 2 * LANES : 3 * LANES])
            sig = jax.nn.sigmoid(gate)
            hidden = (gate * sig * up).astype(BF)
            grad_gate = (hidden_grad * up * sig * (1.0 + gate * (1.0 - sig))).astype(BF)
            grad_up = (hidden_grad * gate * sig).astype(BF)
            first = 3 * LANES * piece
            grads_all[block, first : first + LANES] = grad_gate
            grads_all[block, first + LANES : first + 2 * LANES] = grad_up
            grads_all[block, first + 2 * LANES : first + 3 * LANES] = hidden
            both += [grad_gate, grad_up]
            slot = slot + jnp.sum(hidden.astype(F32) * hidden_grad, axis=1, keepdims=True)
        grads = jnp.concatenate(both, axis=1)
        for pair in range(pairs):
            rows = dot(grads, gu_wt[:, 2 * LANES * pair : 2 * LANES * (pair + 1)]).astype(BF)
            for side in range(2):
                chunk = 2 * pair + side
                part = rows[:, side * LANES : (side + 1) * LANES]
                back[at, :, chunk] = part[0:MAIN].reshape(LINE, ROWS, LANES)
                stack[chunk * FOLD : (chunk + 1) * FOLD] = part[MAIN:QROWS]
        which = lax.broadcasted_iota(jnp.int32, (QROWS, LANES), 0)
        lane = lax.broadcasted_iota(jnp.int32, (QROWS, LANES), 1)
        wanted = jnp.where(which < MAIN, lax.rem(which, ROWS), ROWS)
        spots = jnp.where(lane == wanted, slot, 0.0)
        high = spots.astype(BF)
        low = (spots - high.astype(F32)).astype(BF)
        folded = dot(spread_t[...], stack[...]) + dot(place[0], high) + dot(place[1], low)
        back[at, :, chunks] = folded.astype(BF).reshape(LINE, ROWS, LANES)

    transposed(0)
    for piece in range(len(pieces)):
        weight_copy(1, piece).wait_recv()
        weight_copy(2, piece).start()
    relay_hop(0)
    for q in (2, 1, 3, 0):
        gather_hop(q, 1)
    for piece in range(len(pieces)):
        weight_copy(2, piece).wait_recv()
        weight_copy(3, piece).start()
    relay_hop(1)
    for q in (2, 1, 3, 0):
        gather_hop(q, 2)
    weight_copy(0, 0).wait_recv()
    core_copy(0).start()
    for piece in range(len(pieces)):
        weight_copy(3, piece).wait_recv()
    core_copy(1).start()
    relay_hop(2)
    for q in (2, 1, 3, 0):
        gather_hop(q, 3)
    for number in range(2):
        core_copy(number).wait_recv()
    transposed(1)
    relay_hop(3)

    def quarter(step, carry):
        q = step + lax.div(step, 2) * (5 - 2 * step)

        @pl.when(q > 0)
        def _():
            for kind in range(2):
                for slot in range(LINE):
                    y_copy(q, kind, slot).wait_recv()

        compute_rows(q)

        @pl.when(step == 0)
        def _():
            reduce_level(0, 0)

        @pl.when((step == 1) | (step == 2))
        def _():
            for slot in range(LINE):
                r_copy(q, slot).start()

        @pl.when(step == 3)
        def _():
            for slot in range(LINE):
                r_half(slot).start()

        @pl.when(step == 1)
        def _():
            reduce_level(0, 1)

        @pl.when(step == 2)
        def _():
            returned(1)
            reduce_level(1, 0)
            reduce_level(0, 2)

        @pl.when(step == 3)
        def _():
            returned(3)
            reduce_level(3, 0)
            reduce_level(1, 1)

        return carry

    lax.fori_loop(0, NY, quarter, 0)

    width = 4 * LANES
    grads_t[...] = grads_all[...].T

    def weight_terms(piece, target):
        first = 3 * LANES * piece
        for start in range(0, features, width):
            span = slice(start, start + width)
            target[0 : 2 * LANES, span] = dot(grads_t[first : first + 2 * LANES], x_all[:, span]).astype(BF)
            target[2 * LANES : 3 * LANES, span] = dot(grads_t[first + 2 * LANES : first + 3 * LANES], c_all[:, span]).astype(BF)

    weight_terms(1, mirror_grad)
    core_copy(2).start()
    for slot in range(LINE):
        r_half(slot).wait_recv()
        r_rest(slot).start()
    reduce_level(1, 2)
    reduce_level(3, 1)
    core_copy(2).wait_recv()
    mine = rows_at(0, half)
    mirror_grad[:, mine] = (mirror_grad[:, mine].astype(F32) + mirror_half[...].astype(F32)).astype(BF)
    for piece in range(len(pieces)):
        grad_copy(1, piece).start()
    grad_copy(0, 0).start()
    returned(2)
    reduce_level(2, 0)
    weight_terms(0, own_grad)
    core_copy(2).wait_send()
    core_copy(3).start()
    reduce_level(3, 2)
    for piece in range(len(pieces)):
        grad_copy(1, piece).wait_recv()
        grad_copy(2, piece).start()
    reduce_level(2, 1)
    for q in (0, 1):
        reduce_end(q)
    reduce_level(2, 2)
    for piece in range(len(pieces)):
        grad_copy(2, piece).wait_recv()
        grad_copy(3, piece).start()
    for q in (3, 2):
        reduce_end(q)

    col, slot_col, _, code_col = codes()
    unpick = one_hot(code_col, (count, MAIN), 1)
    unpick_fold = one_hot(code_col, (count, FOLD), 1, MAIN)
    folded = ret[:, chunks].reshape(MAIN, LANES)
    unfolded = dot(spread[...], folded).astype(BF)
    for chunk in range(chunks):
        rows = ret[:, chunk].reshape(MAIN, LANES)
        total = dot(unpick, rows) + dot(unpick_fold, unfolded[chunk * FOLD : (chunk + 1) * FOLD])
        token_out[:, chunk * LANES : (chunk + 1) * LANES] = total.astype(BF)
    lane = lax.broadcasted_iota(jnp.int32, (count, LANES), 1).astype(F32)
    total = jnp.zeros((count, LANES), F32)
    for q in range(NY):
        last = ret[q, chunks].astype(F32)
        entry = last[HIGH : HIGH + 1] + last[LOW : LOW + 1]
        total = total + jnp.where((lane == slot_col) & (col == q), entry, 0.0)
    slot_sum = jnp.sum(total, axis=1, keepdims=True)
    first = lax.broadcasted_iota(jnp.int32, (count, count), 0)
    second = lax.broadcasted_iota(jnp.int32, (count, count), 1)
    sum_row = jnp.sum(jnp.where(first == second, slot_sum, 0.0), axis=0, keepdims=True)
    route_out[...] = (sum_row / route_row[...].astype(F32)).astype(BF)

    core_copy(3).wait_recv()
    grad_copy(0, 0).wait_recv()
    for piece in range(len(pieces)):
        grad_copy(3, piece).wait_recv()
    grad_copy(0, 0).wait_send()
    for piece in range(len(pieces)):
        grad_copy(1, piece).wait_send()
    grad_out[:, mine] = (own_grad[:, mine].astype(F32) + own_half[...].astype(F32) + far_half[...].astype(F32)).astype(BF)
    core_copy(4).start()
    core_copy(4).wait_recv()

    for number in (0, 1, 3, 4):
        core_copy(number).wait_send()
    weight_copy(0, 0).wait_send()
    for piece in range(len(pieces)):
        weight_copy(1, piece).wait_send()
        for leg in (2, 3):
            weight_copy(leg, piece).wait_send()
            grad_copy(leg, piece).wait_send()
    for q in range(NY):
        place_at = position(q)
        for slot in range(LINE):
            for kind in range(2):
                if q > 0:
                    y_copy(q, kind, slot).wait_send()

                @pl.when((slot <= place_at) & (place_at < LINE - 1))
                def _():
                    ag_copy(q, kind, 0, slot).wait_send()

                @pl.when((slot >= place_at) & (place_at > 0))
                def _():
                    ag_copy(q, kind, 1, slot).wait_send()

            if q > 0:
                r_copy(q, slot).wait_send()
            if q < 2:
                y_rest(q, slot).wait_send()
            if q == 2:
                r_rest(slot).wait_send()
            if slot > 0:

                @pl.when(place_at < slot)
                def _():
                    rs_copy(q, 0, slot).wait_send()

            if slot < LINE - 1:

                @pl.when(place_at > slot)
                def _():
                    rs_copy(q, 1, slot).wait_send()


def shards(tokens, expert_ids, route_weight, cotangent, w_gate, w_up, w_down):
    count, features = tokens.shape[1:]
    hidden = w_gate.shape[2]
    chunks = features // LANES
    spread, spread_t, place = fold_matrices(chunks)
    vmem = pl.BlockSpec(memory_space=pltpu.VMEM)
    anywhere = pl.BlockSpec(memory_space=pl.ANY)
    message = (chunks + 1, ROWS, LANES)
    half = features // 2
    dma = pltpu.SemaphoreType.DMA
    token_grad, route_grad, weight_grad = pl.pallas_call(
        kernel,
        out_shape=(
            jax.ShapeDtypeStruct((count, features), BF),
            jax.ShapeDtypeStruct((1, count), BF),
            jax.ShapeDtypeStruct((3 * hidden, features), BF),
        ),
        in_specs=[vmem] * 2 + [anywhere] * 5 + [vmem] * 3,
        out_specs=(vmem, vmem, vmem),
        scratch_shapes=[
            pltpu.VMEM((7, 2, LINE) + message, BF),
            pltpu.VMEM((7, LINE) + message, BF),
            pltpu.VMEM((NY, 2, LINE - 1) + message, BF),
            pltpu.VMEM((2, LINE) + message, BF),
            pltpu.VMEM((LINE,) + message, BF),
            pltpu.VMEM((NY,) + message, BF),
            pltpu.VMEM((2, features, 3 * hidden), BF),
            pltpu.VMEM((4 * hidden, features), BF),
            pltpu.VMEM((NY * QROWS, features), BF),
            pltpu.VMEM((NY * QROWS, features), BF),
            pltpu.VMEM((NY * QROWS, 6 * hidden), BF),
            pltpu.VMEM((6 * hidden, NY * QROWS), BF),
            pltpu.VMEM((half // 2, 3 * hidden), BF),
            pltpu.VMEM((half // 2, 3 * hidden), BF),
            pltpu.VMEM((3 * hidden, half), BF),
            pltpu.VMEM((3 * hidden, half), BF),
            pltpu.VMEM((3 * hidden, half), BF),
            pltpu.VMEM((3 * hidden, half // 2), BF),
            pltpu.VMEM((3 * hidden, half // 2), BF),
            pltpu.VMEM((chunks * FOLD, LANES), BF),
            dma((5,)),
            dma((NY, 2, 2, LINE)),
            dma((NY, 2, LINE)),
            dma((NY, 2, LINE)),
            dma((NY, 2, LINE)),
            dma((3, LINE)),
            dma((3, LINE)),
            dma((NY, LINE)),
            dma((NY, LINE)),
            dma((NY, 2, LINE)),
            dma((NY, 2, LINE)),
            dma((13,)),
            dma((13,)),
            dma((13,)),
            dma((13,)),
            dma((5,)),
            dma((5,)),
        ],
        compiler_params=pltpu.CompilerParams(
            collective_id=0, has_side_effects=True, vmem_limit_bytes=63 * 1024 * 1024
        ),
        cost_estimate=pl.CostEstimate(flops=8_000_000_000, bytes_accessed=10_000_000, transcendentals=140_000),
    )(
        expert_ids.reshape(1, count), route_weight.reshape(1, count), tokens[0], cotangent[0],
        w_gate[0], w_up[0], w_down[0], spread, spread_t, place,
    )
    grad_gate = weight_grad[0:hidden].T
    grad_up = weight_grad[hidden : 2 * hidden].T
    grad_down = weight_grad[2 * hidden : 3 * hidden]
    return (token_grad[None], route_grad.reshape(1, count, 1), grad_gate[None], grad_up[None], grad_down[None])


def solution(mesh):
    rows = P("pipe", "expert", None)
    columns = P("pipe", None, "expert")
    return jax.shard_map(
        shards, mesh=mesh,
        in_specs=(rows, rows, rows, rows, columns, columns, rows),
        out_specs=(rows, rows, columns, columns, rows),
        check_vma=False,
    )
```

```python
import jax
import jax.numpy as jnp
import numpy as np
from jax import lax
from jax.experimental import pallas as pl
from jax.experimental.pallas import tpu as pltpu
from jax.sharding import PartitionSpec as P

MESH = pl.DeviceIdType.MESH
BF = jnp.bfloat16
F32 = jnp.float32
ROWS = 32
LANES = 128
FOLD = 16
HIGH, LOW = 28, 29
NY, NZ, LINE = 4, 8, 4
MAIN = LINE * ROWS
QROWS = MAIN + FOLD


def dot(left, right):
    return jnp.dot(left, right, preferred_element_type=F32)


def fold_matrices(chunks):
    spread = np.zeros((chunks * FOLD, MAIN), np.float32)
    for chunk in range(chunks):
        for slot in range(LINE):
            spread[chunk * FOLD + slot, slot * ROWS + chunk] = 1.0
    place = np.zeros((2, MAIN, QROWS), np.float32)
    for part, row in ((0, HIGH), (1, LOW)):
        for slot in range(LINE):
            place[part, slot * ROWS + row, slot * ROWS : (slot + 1) * ROWS] = 1.0
            place[part, slot * ROWS + row, MAIN + slot] = 1.0
    return jnp.asarray(spread, BF), jnp.asarray(spread.T, BF), jnp.asarray(place, BF)


def kernel(
    ids_row, route_row, tokens_in, cot_in, w_gate, w_up, w_down_in, spread, spread_t, place,
    token_out, route_out, grad_out,
    buf, back, ring, relay, back_relay, ret, w_nat, gu_wt, x_all, c_all, grads_all, grads_t, relay_in, relay_on,
    mirror_half, own_half, far_half, grad_in, grad_on, stack,
    w_sem, ag_send, ag_recv, y_send, y_recv, relay_send, relay_recv, r_send, r_recv, rs_send, rs_recv,
    m_send, m_recv, d_send, d_recv, c_send, c_recv,
):
    count, features = tokens_in.shape
    tokens, cot, w_down = (x_all.at[index * count : (index + 1) * count] for index in range(3))
    mirror_grad, own_grad = grad_out, gu_wt.at[0 : 3 * LANES]
    chunks = features // LANES
    pairs = chunks // 2
    half = features // 2
    direct = half // 2
    direct_back = direct
    pieces = tuple((start, min(2 * LANES, half - start)) for start in range(direct, half, 2 * LANES))
    pieces_back = tuple((start, min(2 * LANES, half - start)) for start in range(direct_back, half, 2 * LANES))
    me_p = lax.axis_index("pipe")
    me_e = lax.axis_index("expert")
    plane = lax.div(me_p, 2)
    core = lax.rem(me_p, 2)
    y = lax.div(me_e, NZ)
    z = lax.rem(me_e, NZ)
    turn = lax.rem(y + 2 * plane, LINE)
    right = (me_p, y * NZ + lax.rem(z + 1, NZ))
    left = (me_p, y * NZ + lax.rem(z + NZ - 1, NZ))
    partner = (me_p + 1 - 2 * core, me_e)
    planes = lax.axis_size("pipe") // 2
    beside = tuple((2 * lax.rem(plane + apart, planes) + core, me_e) for apart in (1, planes - 1))
    mirror = (me_p, y * NZ + lax.rem(2 * turn + 7 - z + NZ, NZ))
    mirror_on = (me_p, y * NZ + lax.rem(2 * lax.rem(turn + 2, LINE) + 7 - z + NZ, NZ))
    ring_to = (right, left)
    base = core * half
    away = half - base

    def y_device(apart):
        return (me_p, lax.rem(y + apart, NY) * NZ + z)

    def position(q):
        return lax.rem(z + LINE - lax.rem(turn + q, LINE), LINE)

    def landed(q):
        return q + 3 - 3 * lax.div(3 - q, 3)

    def remote(source, target, send, recv, device):
        return pltpu.make_async_remote_copy(
            src_ref=source, dst_ref=target, send_sem=send, recv_sem=recv, device_id=device, device_id_type=MESH
        )

    def ag_copy(q, kind, way, slot):
        at = buf.at[q, kind, slot]
        return remote(at, at, ag_send.at[q, kind, way, slot], ag_recv.at[q, kind, slot], ring_to[way])

    def y_copy(q, kind, slot):
        return remote(buf.at[q, kind, slot], buf.at[q + 3, kind, slot], y_send.at[q, kind, slot], y_recv.at[q, kind, slot], y_device(q))

    def y_half(kind, slot):
        return remote(buf.at[2, kind, slot], relay.at[kind, slot], y_send.at[2, kind, slot], relay_recv.at[kind, slot], y_device(1 + 2 * kind))

    def y_rest(kind, slot):
        return remote(relay.at[kind, slot], buf.at[5, kind, slot], relay_send.at[kind, slot], y_recv.at[2, kind, slot], y_device(1 + 2 * kind))

    def r_half(slot):
        return remote(back.at[5, slot], back_relay.at[slot], r_send.at[2, slot], relay_recv.at[2, slot], y_device(1 + slot // 2 * 2))

    def r_rest(slot):
        return remote(back_relay.at[slot], back.at[2, slot], relay_send.at[2, slot], r_recv.at[2, slot], y_device(1 + slot // 2 * 2))

    def y_start(q, kind, slot):
        if q == 2:
            y_half(kind, slot).start()
        elif q > 0:
            y_copy(q, kind, slot).start()

    def relay_hop(hop):
        for kind in range(2):
            place_at = position(1 + 2 * kind)

            def onward(slot):
                y_half(kind, slot).wait_recv()
                y_rest(kind, slot).start()

            if hop == 0:
                onward(place_at)
                continue

            @pl.when(place_at >= hop)
            def _():
                onward(place_at - hop)

            @pl.when(place_at + hop < LINE)
            def _():
                onward(place_at + hop)

    def r_copy(q, slot):
        return remote(back.at[q + 3, slot], back.at[q, slot], r_send.at[q, slot], r_recv.at[q, slot], y_device(NY - q))

    def rs_copy(q, way, slot):
        return remote(back.at[q, slot], ring.at[q, way, slot - 1 + way], rs_send.at[q, way, slot], rs_recv.at[q, way, slot], ring_to[way])

    def rows_at(offset, size):
        return pl.ds(pl.multiple_of(base + offset, LANES), size)

    def weight_copy(leg, piece):
        if leg == 0:
            span = rows_at(0, direct)
            return remote(w_nat.at[0, span], w_nat.at[1, span], m_send.at[0], m_recv.at[0], mirror)
        offset, size = pieces[piece]
        span, local = rows_at(offset, size), pl.ds(offset - direct, size)
        number = len(pieces) * (leg - 1) + 1 + piece
        there, back_there = beside[piece % 2], beside[1 - piece % 2]
        if leg == 1:
            return remote(w_nat.at[0, span], relay_in.at[local], m_send.at[number], m_recv.at[number], there)
        if leg == 2:
            return remote(relay_in.at[local], relay_on.at[local], m_send.at[number], m_recv.at[number], mirror_on)
        return remote(relay_on.at[local], w_nat.at[1, span], m_send.at[number], m_recv.at[number], back_there)

    def grad_copy(leg, piece):
        if leg == 0:
            return remote(mirror_grad.at[:, rows_at(0, direct_back)], far_half.at[:, 0:direct_back], d_send.at[0], d_recv.at[0], mirror)
        offset, size = pieces_back[piece]
        span, local = rows_at(offset, size), pl.ds(offset - direct_back, size)
        number = len(pieces_back) * (leg - 1) + 1 + piece
        there, back_there = beside[piece % 2], beside[1 - piece % 2]
        if leg == 1:
            return remote(mirror_grad.at[:, span], grad_in.at[:, local], d_send.at[number], d_recv.at[number], there)
        if leg == 2:
            return remote(grad_in.at[:, local], grad_on.at[:, local], d_send.at[number], d_recv.at[number], mirror_on)
        return remote(grad_on.at[:, local], far_half.at[:, offset : offset + size], d_send.at[number], d_recv.at[number], back_there)

    def core_copy(number):
        if number < 2:
            span = rows_at(number * direct, direct)
            return remote(w_nat.at[1, span], w_nat.at[1, span], c_send.at[number], c_recv.at[number], partner)
        mine, other = rows_at(0, half), pl.ds(pl.multiple_of(away, LANES), half)
        if number == 2:
            return remote(mirror_grad.at[:, other], mirror_half, c_send.at[2], c_recv.at[2], partner)
        if number == 3:
            return remote(gu_wt.at[0 : 3 * LANES, other], own_half, c_send.at[3], c_recv.at[3], partner)
        return remote(grad_out.at[:, mine], grad_out.at[:, mine], c_send.at[4], c_recv.at[4], partner)

    def codes():
        rel = ids_row[...].astype(F32) - y.astype(F32)
        row = jnp.where(rel < 0, rel + NY, rel)
        first = lax.broadcasted_iota(jnp.int32, (count, count), 0)
        second = lax.broadcasted_iota(jnp.int32, (count, count), 1)
        col = to_column(row)
        same = jnp.where(col == row, 1.0, 0.0)
        slot_row = jnp.sum(jnp.where(first < second, same, 0.0), axis=0, keepdims=True)
        slot_col = jnp.sum(jnp.where(second < first, same, 0.0), axis=1, keepdims=True)
        code_row = jnp.where(slot_row < ROWS, row * ROWS + slot_row, MAIN + row)
        code_col = jnp.where(slot_col < ROWS, col * ROWS + slot_col, MAIN + col)
        return col, slot_col, code_row, code_col

    def to_column(row):
        first = lax.broadcasted_iota(jnp.int32, (count, count), 0)
        second = lax.broadcasted_iota(jnp.int32, (count, count), 1)
        return jnp.sum(jnp.where(first == second, row, 0.0), axis=1, keepdims=True)

    def one_hot(code, shape, dim, start=0):
        places = lax.broadcasted_iota(jnp.int32, shape, dim) + start
        return jnp.where(places.astype(F32) == code, 1.0, 0.0).astype(BF)

    def transposed(piece):
        for chunk in range(chunks):
            span = slice(chunk * LANES, (chunk + 1) * LANES)
            gu_wt[2 * LANES * piece : 2 * LANES * (piece + 1), span] = w_nat[piece, span, 0 : 2 * LANES].T

    loads = (
        pltpu.make_async_copy(w_gate, w_nat.at[0, :, 0:LANES], w_sem.at[0]),
        pltpu.make_async_copy(w_up, w_nat.at[0, :, LANES : 2 * LANES], w_sem.at[1]),
        pltpu.make_async_copy(w_down_in, w_down, w_sem.at[2]),
        pltpu.make_async_copy(tokens_in, tokens, w_sem.at[3]),
        pltpu.make_async_copy(cot_in, cot, w_sem.at[4]),
    )
    for index in (3, 4, 2, 0, 1):
        loads[index].start()
    barrier = pltpu.get_barrier_semaphore()
    for device in (right, left, y_device(1), y_device(2), y_device(3), partner) + beside + (mirror, mirror_on):
        pl.semaphore_signal(barrier, inc=1, device_id=device, device_id_type=MESH)
    def own_start(q, kind):
        place_at = position(q)

        @pl.when(place_at < LINE - 1)
        def _():
            ag_copy(q, kind, 0, place_at).start()

        @pl.when(place_at > 0)
        def _():
            ag_copy(q, kind, 1, place_at).start()

        y_start(q, kind, place_at)

    _, _, code_row, _ = codes()
    pick = one_hot(code_row, (QROWS, count), 0)
    loads[3].wait()
    for kind, values in ((0, tokens), (1, c_all)):
        if kind == 1:
            loads[4].wait()
            c_all[0:count] = (cot[...].astype(F32) * to_column(route_row[...].astype(F32))).astype(BF)
        for pair in range(pairs):
            rows = dot(pick, values[0:count, 2 * LANES * pair : 2 * LANES * (pair + 1)]).astype(BF)
            for side in range(2):
                chunk = 2 * pair + side
                part = rows[:, side * LANES : (side + 1) * LANES]
                for q in range(NY):
                    buf[q, kind, position(q), chunk] = part[q * ROWS : (q + 1) * ROWS]
                stack[chunk * FOLD : (chunk + 1) * FOLD] = part[MAIN:QROWS]
        folded = dot(spread_t[...], stack[...]).astype(BF)
        for q in range(NY):
            buf[q, kind, position(q), chunks] = folded[q * ROWS : (q + 1) * ROWS]
        if kind == 0:
            pl.semaphore_wait(barrier, 10)
        for q in (2, 1, 3, 0):
            own_start(q, kind)
    loads[2].wait()
    for chunk in range(chunks):
        span = slice(chunk * LANES, (chunk + 1) * LANES)
        w_nat[0, span, 2 * LANES : 3 * LANES] = w_down[:, span].T
    for index in (0, 1):
        loads[index].wait()
    for piece in range(len(pieces)):
        weight_copy(1, piece).start()

    def gather_hop(q, hop):
        place_at = position(q)

        def one_kind(kind, carry):
            def arrived(way, slot, onward):
                ag_copy(q, kind, way, slot).wait_recv()

                @pl.when(onward)
                def _():
                    ag_copy(q, kind, way, slot).start()

                y_start(q, kind, slot)

            @pl.when(place_at >= hop)
            def _():
                arrived(0, place_at - hop, place_at < LINE - 1)

            @pl.when(place_at + hop < LINE)
            def _():
                arrived(1, place_at + hop, place_at > 0)

            return carry

        lax.fori_loop(0, 2, one_kind, 0)

    def merge(first, second):
        total = first.astype(F32) + second.astype(F32)
        sums = total[HIGH : HIGH + 1] + total[LOW : LOW + 1]
        high = sums.astype(BF).astype(F32)
        row = lax.broadcasted_iota(jnp.int32, (ROWS, LANES), 0)
        return jnp.where(row == HIGH, high, jnp.where(row == LOW, sums - high, total)).astype(BF)

    def add_message(target, first, second):
        target[0:chunks] = (first[0:chunks].astype(F32) + second[0:chunks].astype(F32)).astype(BF)
        target[chunks] = merge(first[chunks], second[chunks])

    def reduce_level(q, level):
        place_at = position(q)

        def step(way, slot, came):
            if level > 0:
                rs_copy(q, way, slot).wait_recv()
                add_message(back.at[q, slot], back.at[q, slot], ring.at[q, way, came])
            rs_copy(q, way, slot).start()

        @pl.when(place_at == level)
        def _():
            for slot in range(LINE - 1, level, -1):
                step(0, slot, slot - 1)

        @pl.when(place_at == LINE - 1 - level)
        def _():
            for slot in range(LINE - 1 - level):
                step(1, slot, slot)

    def reduce_end(q):
        place_at = position(q)
        ret[q] = back[q, place_at]

        @pl.when(place_at > 0)
        def _():
            rs_copy(q, 0, place_at).wait_recv()
            add_message(ret.at[q], ret.at[q], ring.at[q, 0, place_at - 1])

        @pl.when(place_at < LINE - 1)
        def _():
            rs_copy(q, 1, place_at).wait_recv()
            add_message(ret.at[q], ret.at[q], ring.at[q, 1, place_at])

    def returned(q):
        for slot in range(LINE):
            r_copy(q, slot).wait_recv()

    def compute_rows(q):
        at = landed(q)
        start = q * QROWS
        block = pl.ds(pl.multiple_of(start, FOLD), QROWS)
        for kind, rows in ((0, x_all), (1, c_all)):
            folded = buf[at, kind, :, chunks].reshape(MAIN, LANES)
            unfolded = dot(spread[...], folded).astype(BF)
            for chunk in range(chunks):
                span = slice(chunk * LANES, (chunk + 1) * LANES)
                rows[pl.ds(pl.multiple_of(start, FOLD), MAIN), span] = buf[at, kind, :, chunk].reshape(MAIN, LANES)
                rows[pl.ds(pl.multiple_of(start + MAIN, FOLD), FOLD), span] = unfolded[chunk * FOLD : (chunk + 1) * FOLD]
        slot = jnp.zeros((QROWS, 1), F32)
        both = []
        for piece in range(2):
            pre = dot(x_all[block], w_nat[piece, :, 0 : 2 * LANES])
            gate, up = pre[:, 0:LANES], pre[:, LANES : 2 * LANES]
            hidden_grad = dot(c_all[block], w_nat[piece, :, 2 * LANES : 3 * LANES])
            sig = jax.nn.sigmoid(gate)
            hidden = (gate * sig * up).astype(BF)
            grad_gate = (hidden_grad * up * sig * (1.0 + gate * (1.0 - sig))).astype(BF)
            grad_up = (hidden_grad * gate * sig).astype(BF)
            first = 3 * LANES * piece
            grads_all[block, first : first + LANES] = grad_gate
            grads_all[block, first + LANES : first + 2 * LANES] = grad_up
            grads_all[block, first + 2 * LANES : first + 3 * LANES] = hidden
            both += [grad_gate, grad_up]
            slot = slot + jnp.sum(hidden.astype(F32) * hidden_grad, axis=1, keepdims=True)
        grads = jnp.concatenate(both, axis=1)
        for pair in range(pairs):
            rows = dot(grads, gu_wt[:, 2 * LANES * pair : 2 * LANES * (pair + 1)]).astype(BF)
            for side in range(2):
                chunk = 2 * pair + side
                part = rows[:, side * LANES : (side + 1) * LANES]
                back[at, :, chunk] = part[0:MAIN].reshape(LINE, ROWS, LANES)
                stack[chunk * FOLD : (chunk + 1) * FOLD] = part[MAIN:QROWS]
        which = lax.broadcasted_iota(jnp.int32, (QROWS, LANES), 0)
        lane = lax.broadcasted_iota(jnp.int32, (QROWS, LANES), 1)
        wanted = jnp.where(which < MAIN, lax.rem(which, ROWS), ROWS)
        spots = jnp.where(lane == wanted, slot, 0.0)
        high = spots.astype(BF)
        low = (spots - high.astype(F32)).astype(BF)
        folded = dot(spread_t[...], stack[...]) + dot(place[0], high) + dot(place[1], low)
        back[at, :, chunks] = folded.astype(BF).reshape(LINE, ROWS, LANES)

    transposed(0)
    relay_hop(0)
    for q in (2, 1, 3, 0):
        gather_hop(q, 1)
    relay_hop(1)
    for q in (2, 1, 3, 0):
        gather_hop(q, 2)
    weight_copy(0, 0).start()
    for piece in range(len(pieces)):
        weight_copy(1, piece).wait_recv()
        weight_copy(2, piece).start()
    relay_hop(2)
    for q in (2, 1, 3, 0):
        gather_hop(q, 3)
    for piece in range(len(pieces)):
        weight_copy(2, piece).wait_recv()
        weight_copy(3, piece).start()
    relay_hop(3)
    weight_copy(0, 0).wait_recv()
    core_copy(0).start()
    for piece in range(len(pieces)):
        weight_copy(3, piece).wait_recv()
    core_copy(1).start()
    for number in range(2):
        core_copy(number).wait_recv()
    transposed(1)

    def quarter(step, carry):
        q = step + lax.div(step, 2) * (5 - 2 * step)

        @pl.when(q > 0)
        def _():
            for kind in range(2):
                for slot in range(LINE):
                    y_copy(q, kind, slot).wait_recv()

        compute_rows(q)

        @pl.when(step == 0)
        def _():
            reduce_level(0, 0)

        @pl.when((step == 1) | (step == 2))
        def _():
            for slot in range(LINE):
                r_copy(q, slot).start()

        @pl.when(step == 3)
        def _():
            for slot in range(LINE):
                r_half(slot).start()

        @pl.when(step == 1)
        def _():
            reduce_level(0, 1)

        @pl.when(step == 2)
        def _():
            returned(1)
            reduce_level(1, 0)
            reduce_level(0, 2)

        @pl.when(step == 3)
        def _():
            returned(3)
            reduce_level(3, 0)
            reduce_level(1, 1)

        return carry

    lax.fori_loop(0, NY, quarter, 0)

    grads_t[...] = grads_all[...].T

    def weight_terms(piece, target):
        first = 3 * LANES * piece
        for start in range(0, features, 4 * LANES):
            span = slice(start, start + 4 * LANES)
            target[0 : 2 * LANES, span] = dot(grads_t[first : first + 2 * LANES], x_all[:, span]).astype(BF)
            target[2 * LANES : 3 * LANES, span] = dot(grads_t[first + 2 * LANES : first + 3 * LANES], c_all[:, span]).astype(BF)

    weight_terms(1, mirror_grad)
    core_copy(2).start()
    reduce_level(1, 2)
    reduce_level(3, 1)
    core_copy(2).wait_recv()
    mine = rows_at(0, half)
    for piece, (offset, size) in enumerate(pieces_back + ((0, direct_back),)):
        span = rows_at(offset, size)
        mirror_grad[:, span] = (mirror_grad[:, span].astype(F32) + mirror_half[:, offset : offset + size].astype(F32)).astype(BF)
        grad_copy(*((1, piece) if offset else (0, 0))).start()
    for slot in range(LINE):
        r_half(slot).wait_recv()
        r_rest(slot).start()
    weight_terms(0, own_grad)
    core_copy(2).wait_send()
    core_copy(3).start()
    for piece in range(len(pieces_back)):
        grad_copy(1, piece).wait_recv()
        grad_copy(2, piece).start()
    returned(2)
    reduce_level(2, 0)
    reduce_level(3, 2)
    reduce_level(2, 1)
    for q in (0, 1):
        reduce_end(q)
    reduce_level(2, 2)
    for piece in range(len(pieces_back)):
        grad_copy(2, piece).wait_recv()
        grad_copy(3, piece).start()
    for q in (3, 2):
        reduce_end(q)

    col, slot_col, _, code_col = codes()
    unpick = one_hot(code_col, (count, MAIN), 1)
    unpick_fold = one_hot(code_col, (count, FOLD), 1, MAIN)
    folded = ret[:, chunks].reshape(MAIN, LANES)
    unfolded = dot(spread[...], folded).astype(BF)
    for chunk in range(chunks):
        rows = ret[:, chunk].reshape(MAIN, LANES)
        total = dot(unpick, rows) + dot(unpick_fold, unfolded[chunk * FOLD : (chunk + 1) * FOLD])
        token_out[:, chunk * LANES : (chunk + 1) * LANES] = total.astype(BF)
    lane = lax.broadcasted_iota(jnp.int32, (count, LANES), 1).astype(F32)
    total = jnp.zeros((count, LANES), F32)
    for q in range(NY):
        last = ret[q, chunks].astype(F32)
        entry = last[HIGH : HIGH + 1] + last[LOW : LOW + 1]
        total = total + jnp.where((lane == slot_col) & (col == q), entry, 0.0)
    slot_sum = jnp.sum(total, axis=1, keepdims=True)
    first = lax.broadcasted_iota(jnp.int32, (count, count), 0)
    second = lax.broadcasted_iota(jnp.int32, (count, count), 1)
    sum_row = jnp.sum(jnp.where(first == second, slot_sum, 0.0), axis=0, keepdims=True)
    route_out[...] = (sum_row / route_row[...].astype(F32)).astype(BF)

    core_copy(3).wait_recv()
    grad_copy(0, 0).wait_recv()
    for piece in range(len(pieces_back)):
        grad_copy(3, piece).wait_recv()
    grad_copy(0, 0).wait_send()
    for piece in range(len(pieces_back)):
        grad_copy(1, piece).wait_send()
    grad_out[:, mine] = (own_grad[:, mine].astype(F32) + own_half[...].astype(F32) + far_half[...].astype(F32)).astype(BF)
    core_copy(4).start()
    core_copy(4).wait_recv()

    for number in (0, 1, 3, 4):
        core_copy(number).wait_send()
    weight_copy(0, 0).wait_send()
    for leg in (1, 2, 3):
        for piece in range(len(pieces)):
            weight_copy(leg, piece).wait_send()
    for leg in (2, 3):
        for piece in range(len(pieces_back)):
            grad_copy(leg, piece).wait_send()
    for q in range(NY):
        place_at = position(q)
        for slot in range(LINE):
            for kind in range(2):
                if q > 0:
                    y_copy(q, kind, slot).wait_send()

                @pl.when((slot <= place_at) & (place_at < LINE - 1))
                def _():
                    ag_copy(q, kind, 0, slot).wait_send()

                @pl.when((slot >= place_at) & (place_at > 0))
                def _():
                    ag_copy(q, kind, 1, slot).wait_send()

            if q > 0:
                r_copy(q, slot).wait_send()
            if q < 2:
                y_rest(q, slot).wait_send()
            if q == 2:
                r_rest(slot).wait_send()
            if slot > 0:

                @pl.when(place_at < slot)
                def _():
                    rs_copy(q, 0, slot).wait_send()

            if slot < LINE - 1:

                @pl.when(place_at > slot)
                def _():
                    rs_copy(q, 1, slot).wait_send()


def shards(tokens, expert_ids, route_weight, cotangent, w_gate, w_up, w_down):
    count, features = tokens.shape[1:]
    hidden = w_gate.shape[2]
    chunks = features // LANES
    spread, spread_t, place = fold_matrices(chunks)
    vmem = pl.BlockSpec(memory_space=pltpu.VMEM)
    anywhere = pl.BlockSpec(memory_space=pl.ANY)
    message = (chunks + 1, ROWS, LANES)
    half = features // 2
    dma = pltpu.SemaphoreType.DMA
    token_grad, route_grad, weight_grad = pl.pallas_call(
        kernel,
        out_shape=(
            jax.ShapeDtypeStruct((count, features), BF),
            jax.ShapeDtypeStruct((1, count), BF),
            jax.ShapeDtypeStruct((3 * hidden, features), BF),
        ),
        in_specs=[vmem] * 2 + [anywhere] * 5 + [vmem] * 3,
        out_specs=(vmem, vmem, vmem),
        scratch_shapes=[
            pltpu.VMEM((7, 2, LINE) + message, BF),
            pltpu.VMEM((7, LINE) + message, BF),
            pltpu.VMEM((NY, 2, LINE - 1) + message, BF),
            pltpu.VMEM((2, LINE) + message, BF),
            pltpu.VMEM((LINE,) + message, BF),
            pltpu.VMEM((NY,) + message, BF),
            pltpu.VMEM((2, features, 3 * hidden), BF),
            pltpu.VMEM((4 * hidden, features), BF),
            pltpu.VMEM((NY * QROWS, features), BF),
            pltpu.VMEM((NY * QROWS, features), BF),
            pltpu.VMEM((NY * QROWS, 6 * hidden), BF),
            pltpu.VMEM((6 * hidden, NY * QROWS), BF),
            pltpu.VMEM((half // 2, 3 * hidden), BF),
            pltpu.VMEM((half // 2, 3 * hidden), BF),
            pltpu.VMEM((3 * hidden, half), BF),
            pltpu.VMEM((3 * hidden, half), BF),
            pltpu.VMEM((3 * hidden, half), BF),
            pltpu.VMEM((3 * hidden, half // 2), BF),
            pltpu.VMEM((3 * hidden, half // 2), BF),
            pltpu.VMEM((chunks * FOLD, LANES), BF),
            dma((5,)),
            dma((NY, 2, 2, LINE)),
            dma((NY, 2, LINE)),
            dma((NY, 2, LINE)),
            dma((NY, 2, LINE)),
            dma((3, LINE)),
            dma((3, LINE)),
            dma((NY, LINE)),
            dma((NY, LINE)),
            dma((NY, 2, LINE)),
            dma((NY, 2, LINE)),
            dma((13,)),
            dma((13,)),
            dma((13,)),
            dma((13,)),
            dma((5,)),
            dma((5,)),
        ],
        compiler_params=pltpu.CompilerParams(
            collective_id=0, has_side_effects=True, vmem_limit_bytes=63 * 1024 * 1024
        ),
        cost_estimate=pl.CostEstimate(flops=8_000_000_000, bytes_accessed=10_000_000, transcendentals=140_000),
    )(
        expert_ids.reshape(1, count), route_weight.reshape(1, count), tokens[0], cotangent[0],
        w_gate[0], w_up[0], w_down[0], spread, spread_t, place,
    )
    grad_gate = weight_grad[0:hidden].T
    grad_up = weight_grad[hidden : 2 * hidden].T
    grad_down = weight_grad[2 * hidden : 3 * hidden]
    return (token_grad[None], route_grad.reshape(1, count, 1), grad_gate[None], grad_up[None], grad_down[None])


def solution(mesh):
    rows = P("pipe", "expert", None)
    columns = P("pipe", None, "expert")
    return jax.shard_map(
        shards, mesh=mesh,
        in_specs=(rows, rows, rows, rows, columns, columns, rows),
        out_specs=(rows, rows, columns, columns, rows),
        check_vma=False,
    )
```
